32 devices in a mesh: tm: 16 (over z, x, core), chan: 2 (over y).
Axes of the slice: x: 2, y: 2, z: 4, core: 2. Of those that a mesh axis runs over, the one named last changes fastest.
Arguments:
- raw_traces: bfloat16 [1280, 65536], P('chan', 'tm'), may hold values from -120 to 120
- fir_taps: bfloat16 [128], replicated, may hold values from -0.5 to 0.5
- sources: int32 [512], replicated, may hold values from 0 to 1279, as said below
- dead_flags: int32 [1280], P('chan'), may hold values 0 or 1
Outputs:
- correlations: float32 [512, 8, 1280], P('tm', None, 'chan')
The draws below stay inside these ranges and needn't reach their ends.
Inputs may be any that keep to these rules, and one draw needn't show every extreme that they name: `sources`: 512 distinct channel indices; no group of 640 channels that share c // 640 holds more than 384 of them, and one group holds exactly 384.
All inputs are finite; a program needn't handle non-finite values. No bound on the sum of `dead_flags` on one device may be relied on, other than what follows from the above.
Results may differ from the reference program's by a relative error of at most 0.013.
Values may be sent and summed in bfloat16 or wider, within the bound.
No kernel may reach another device: no remote copies, remote signals or barrier semaphores. Data moves between devices by JAX's collectives and lax.ppermute only.
A program may use at most 64 MiB of HBM per device.

```python
import math
import jax
import jax.numpy as jnp
from jax import lax

CH_DEV = 640
VS = 512
TD = 256
NWIN = 4
NLAG = 8
HW = 32
TAPS = 128
DECIM = 4
CH = 1280
WINDOWS = 64
TRAW = 65536
MOST = 384
N_CHAN = 2


def draw_raw_traces(key, part):
    key_noise, key_chan, key_block = jax.random.split(key, 3)
    chan_scale = jnp.exp(jax.random.uniform(key_chan, (CH, 1, 1), jnp.float32, 0.0, math.log(10.0)))
    block_scale = jnp.exp(jax.random.uniform(key_block, (CH, TRAW // 512, 1), jnp.float32, 0.0, math.log(3.0)))
    noise = jnp.clip(jax.random.normal(key_noise, (CH, TRAW), jnp.float32), -4.0, 4.0)
    scaled = noise.reshape(CH, TRAW // 512, 512) * block_scale * chan_scale
    return scaled.reshape(CH, TRAW).astype(jnp.bfloat16)


def draw_sources(key, part):
    key_groups, key_chans, key_order = jax.random.split(key, 3)
    slot_ids = jnp.arange(VS)
    others = N_CHAN - 1
    remain = jnp.maximum(slot_ids - MOST, 0)
    layout = jnp.where(slot_ids < MOST, 0, 1 + remain % others)
    slot_rank = jnp.where(slot_ids < MOST, slot_ids, remain // others)
    group_perm = jax.random.permutation(key_groups, N_CHAN)
    group = group_perm[layout]
    chan_keys = jax.random.split(key_chans, N_CHAN)
    chan_perm = jax.vmap(lambda one_key: jax.random.permutation(one_key, CH_DEV))(chan_keys)
    channel = group * CH_DEV + chan_perm[group, slot_rank]
    order = jax.random.permutation(key_order, VS)
    return channel[order].astype(jnp.int32)


def touch_ends(values, stream_key, low, top_value):
    longest = values.shape.index(max(values.shape))
    spots = []
    for shift in (0, 1):
        where = [jax.random.randint(jax.random.fold_in(stream_key, axis), (), 0, length) for axis, length in enumerate(values.shape)]
        where[longest] = (where[longest] + shift) % values.shape[longest]
        spots.append(tuple(where))
    return values.at[spots[0]].set(low).at[spots[1]].set(top_value)


def normal_values(own_key, dims, spread, bound, kind=jnp.bfloat16):
    result = spread * jax.random.normal(own_key, dims, jnp.float32)
    return jnp.clip(result, min=-bound, max=bound).astype(kind)


def setup_inputs(seed: int = 0) -> dict:
    keys = jax.random.split(jax.random.key(seed), 5)
    raw_traces = draw_raw_traces(jax.random.fold_in(keys[4], 71), 0)
    fir_taps = normal_values(keys[1], (TAPS,), 0.1, 0.5)
    sources = draw_sources(jax.random.fold_in(keys[4], 71), 0)
    dead_flags = touch_ends((jax.random.randint(keys[3], (CH,), 0, 8) < 1).astype(jnp.int32), jax.random.fold_in(keys[3], 1), 0, 1)
    return dict(raw_traces=raw_traces, fir_taps=fir_taps, sources=sources, dead_flags=dead_flags)


def fir_rows(fir_taps, out_block):
    width = TAPS + DECIM * out_block
    padded_taps = jnp.concatenate([jnp.zeros((1,), jnp.bfloat16), fir_taps, jnp.zeros((width + DECIM - TAPS - 1,), jnp.bfloat16)])
    return jnp.tile(padded_taps, out_block)[:out_block * width].reshape(out_block, width)

def dft_table():
    time_index = jnp.arange(TD)[:, None]
    freq_index = jnp.arange(TD // 2)[None, :]
    phase = time_index * freq_index % TD
    angles = 2.0 * math.pi / TD * phase.astype(jnp.float32)
    return jnp.concatenate([jnp.cos(angles), -jnp.sin(angles)], axis=1).astype(jnp.bfloat16)

def lag_tables():
    lag_shift = jnp.arange(NLAG) - NLAG // 2
    freq_index = jnp.arange(TD // 2)
    phase = lag_shift[:, None] * freq_index[None, :] % TD
    angles = 2.0 * math.pi / TD * phase.astype(jnp.float32)
    return (jnp.cos(angles), jnp.sin(angles))

def band_matrix():
    bin_index = jnp.arange(TD // 2)
    return (jnp.abs(bin_index[:, None] - bin_index[None, :]) <= HW).astype(jnp.float32)

def whiten(spectrum, alive):
    half_bins = TD // 2
    real_part = spectrum[..., :half_bins]
    imag_part = spectrum[..., half_bins:]
    amplitude = jnp.sqrt(real_part * real_part + imag_part * imag_part)
    mean_level = jnp.einsum('cwf,fg->cwg', amplitude, band_matrix(), precision=lax.Precision.HIGHEST) / (2 * HW + 1)
    factor = alive / (mean_level + 1e-06)
    return (spectrum * jnp.concatenate([factor, factor], axis=-1)).astype(jnp.bfloat16)

def rotate(source, gain_scale):
    half_bins = TD // 2
    real_src = source[..., :half_bins].astype(jnp.float32)[:, None]
    imag_src = source[..., half_bins:].astype(jnp.float32)[:, None]
    cos_lag, sin_lag = lag_tables()
    cos_lag = cos_lag[None, :, None, :]
    sin_lag = sin_lag[None, :, None, :]
    real_out = (real_src * cos_lag + imag_src * sin_lag) * gain_scale
    imag_out = (imag_src * cos_lag - real_src * sin_lag) * gain_scale
    return jnp.concatenate([real_out, imag_out], axis=-1).astype(jnp.bfloat16)

def decimate(raw_block, fir_taps):
    out_block = min(128, NWIN * TD)
    sample_block = DECIM * out_block
    row_count = raw_block.shape[0]
    grouped = raw_block.reshape(row_count, -1, sample_block)
    before = jnp.concatenate([jnp.zeros((row_count, 1, TAPS), jnp.bfloat16), grouped[:, :-1, sample_block - TAPS:]], axis=1)
    window = jnp.concatenate([before, grouped], axis=2).reshape(-1, TAPS + sample_block)
    matrix = fir_rows(fir_taps, out_block)
    dec = jnp.dot(window.astype(jnp.float32), matrix.T.astype(jnp.float32), preferred_element_type=jnp.float32)
    return dec.astype(jnp.bfloat16).reshape(row_count, -1)

def spectra(raw_block, dead_block, fir_taps):
    dec = decimate(raw_block, fir_taps)
    row_count = dec.shape[0]
    spectrum = jnp.dot(dec.reshape(-1, TD).astype(jnp.float32), dft_table().astype(jnp.float32), preferred_element_type=jnp.float32)
    spectrum = spectrum.reshape(row_count, -1, TD)
    alive = (1 - dead_block).astype(jnp.float32)[:, None, None]
    return whiten(spectrum, alive)

def reference(raw_traces, fir_taps, sources, dead_flags):
    block_count = CH // CH_DEV

    def prepare(segment):
        raw_block, dead_block = segment
        return spectra(raw_block, dead_block, fir_taps)
    whitened = lax.map(prepare, (raw_traces.reshape(block_count, CH_DEV, TRAW), dead_flags.reshape(block_count, CH_DEV)))
    whitened = whitened.reshape(CH, WINDOWS, TD)
    source = jnp.take(whitened, sources, axis=0)
    gain_scale = 1.0 / math.sqrt(WINDOWS * TD)
    seg_count = WINDOWS // NWIN
    white_seg = whitened.reshape(CH, seg_count, NWIN * TD).transpose(1, 0, 2)
    source_seg = source.reshape(VS, seg_count, NWIN, TD).transpose(1, 0, 2, 3)

    def add_segment(stacked, segment):
        src_part, white_part = segment
        lagged = rotate(src_part, gain_scale).reshape(VS * NLAG, NWIN * TD)
        partial_value = jnp.dot(lagged.astype(jnp.float32), white_part.T.astype(jnp.float32), preferred_element_type=jnp.float32)
        rounded = lax.optimization_barrier(partial_value.astype(jnp.bfloat16))
        return (stacked + rounded.astype(jnp.float32), None)
    stacked, unused = lax.scan(add_segment, jnp.zeros((VS * NLAG, CH), jnp.float32), (source_seg, white_seg))
    return stacked.reshape(VS, NLAG, CH)
```

```python
import functools
import math

import jax
import jax.numpy as jnp
import numpy as np
from jax import lax
from jax.experimental import pallas as pl
from jax.experimental.pallas import tpu as pltpu
from jax.sharding import PartitionSpec as P

VS = 512
TD = 256
HALF = TD // 2
NLAG = 8
HW = 32
TAPS = 128
DECIM = 4
SPAN = DECIM * TD
VMEM_LIMIT = 50 * 1024 * 1024
CHUNKS = (8, 8, 8, 8)
ROW_BLOCK = 320

VMEM = pl.BlockSpec(memory_space=pltpu.VMEM)
ANY = pl.BlockSpec(memory_space=pl.ANY)


def params():
    return pltpu.CompilerParams(vmem_limit_bytes=VMEM_LIMIT)


def cost(flops, nbytes):
    return pl.CostEstimate(flops=int(flops), bytes_accessed=int(nbytes), transcendentals=0)


def swap(value, axis, bit):
    return lax.ppermute(value, axis, [(i, i ^ bit) for i in range(lax.axis_size(axis))])


def dft_table():
    phase = np.arange(TD)[:, None] * np.arange(HALF)[None, :] % TD
    angles = np.float32(2.0 * math.pi / TD) * phase.astype(np.float32)
    return np.concatenate([np.cos(angles), -np.sin(angles)], axis=1).astype(jnp.bfloat16)


def lag_tables(gain):
    phase = (np.arange(NLAG) - NLAG // 2)[:, None] * np.arange(HALF)[None, :] % TD
    angles = 2.0 * math.pi / TD * phase.astype(np.float64)
    return (gain * np.cos(angles)).astype(np.float32), (gain * np.sin(angles)).astype(np.float32)


def band_table():
    bins = np.arange(HALF)
    band = (np.abs(bins[:, None] - bins[None, :]) <= HW).astype(np.float32)
    return np.concatenate([band, band], axis=0).astype(jnp.bfloat16)


def fir_base(fir_taps):
    rows = TAPS // DECIM
    width = 2 * TAPS
    padded = jnp.concatenate(
        [jnp.zeros((1,), jnp.bfloat16), fir_taps, jnp.zeros((width + DECIM - TAPS - 1,), jnp.bfloat16)]
    )
    return jnp.tile(padded, rows)[: rows * width].reshape(rows, width)


def nt_dot(left, right):
    return lax.dot_general(left, right, (((1,), (1,)), ((), ())), preferred_element_type=jnp.float32)


def fill_fir(base_ref, fir_ref):
    rows = TAPS // DECIM
    fir_ref[...] = jnp.zeros_like(fir_ref)
    for i in range(TD // rows):
        fir_ref[rows * i : rows * (i + 1), TAPS * i : TAPS * (i + 2)] = base_ref[...]


def whiten_rows(samples, fir_ref, table_ref, band_ref, alive):
    dec = nt_dot(samples, fir_ref[...]).astype(jnp.bfloat16)
    spectrum = jnp.dot(dec, table_ref[...], preferred_element_type=jnp.float32)
    real_part = spectrum[:, :HALF]
    imag_part = spectrum[:, HALF:]
    amplitude = jnp.sqrt(real_part * real_part + imag_part * imag_part)
    high = amplitude.astype(jnp.bfloat16)
    low = (amplitude - high.astype(jnp.float32)).astype(jnp.bfloat16)
    total = jnp.dot(
        jnp.concatenate([high, low], axis=1), band_ref[...], preferred_element_type=jnp.float32
    )
    factor = alive / (total * (1.0 / (2 * HW + 1)) + 1e-06)
    return jnp.concatenate([real_part * factor, imag_part * factor], axis=1).astype(jnp.bfloat16)


def late_kernel(row_block, raw_ref, base_ref, table_ref, band_ref, alive_ref, out_ref, fir_ref, held_ref, sems):
    windows = out_ref.shape[1] // TD
    rows = raw_ref.shape[0]
    first = SPAN - TAPS
    copies = []
    for w in range(windows):
        start = 0 if w == 0 else TAPS + w * SPAN
        stop = TAPS + (w + 1) * SPAN
        copy = pltpu.make_async_copy(
            raw_ref.at[:, first + start : first + stop], held_ref.at[:, start:stop], sems.at[w]
        )
        copy.start()
        copies.append(copy)
    fill_fir(base_ref, fir_ref)
    for w in range(windows):
        copies[w].wait()
        for r in range(0, rows, row_block):
            part = pl.ds(r, row_block)
            out_ref[part, w * TD : (w + 1) * TD] = whiten_rows(
                held_ref[part, w * SPAN : (w + 1) * SPAN + TAPS],
                fir_ref, table_ref, band_ref, alive_ref[part, :],
            )


def first_kernel(
    row_block, sizes, raw_ref, hist_ref, base_ref, table_ref, band_ref, alive_ref, late_ref, sel_ref, *refs
):
    panels = refs[: 2 * len(sizes)]
    white_ref, fir_ref, held_ref, sem = refs[2 * len(sizes) :]
    rows = raw_ref.shape[0]
    copy = pltpu.make_async_copy(raw_ref.at[:, :SPAN], held_ref, sem)
    copy.start()
    fill_fir(base_ref, fir_ref)
    white_ref[:, TD:] = late_ref[...]
    copy.wait()
    for r in range(0, rows, row_block):
        part = pl.ds(r, row_block)
        samples = jnp.concatenate([hist_ref[part, :], held_ref[part, :]], axis=1)
        white_ref[part, :TD] = whiten_rows(samples, fir_ref, table_ref, band_ref, alive_ref[part, :])
    row = 0
    for panel in panels:
        count = panel.shape[0]
        panel[...] = jnp.dot(
            sel_ref[row : row + count, :], white_ref[...], preferred_element_type=jnp.float32
        ).astype(jnp.bfloat16)
        row += count


def main_kernel(own_ref, own_in_ref, sib_ref, sib_in_ref, white_ref, white_sib_ref, cos_ref, sin_ref, keep_ref, send_ref, lag_ref):
    count, depth = own_ref.shape
    cos_lag = cos_ref[...][None]
    sin_lag = sin_ref[...][None]
    for side, (a_ref, b_ref) in enumerate(((own_ref, own_in_ref), (sib_ref, sib_in_ref))):
        for w in range(0, depth, TD):
            parts = []
            for k in (w, w + HALF):
                parts.append(a_ref[:, k : k + HALF].astype(jnp.float32) + b_ref[:, k : k + HALF].astype(jnp.float32))
            real_src, imag_src = (part[:, None, :] for part in parts)
            real_out = real_src * cos_lag + imag_src * sin_lag
            imag_out = imag_src * cos_lag - real_src * sin_lag
            k = side * depth + w
            lag_ref[:, k : k + HALF] = real_out.reshape(count * NLAG, HALF).astype(jnp.bfloat16)
            lag_ref[:, k + HALF : k + TD] = imag_out.reshape(count * NLAG, HALF).astype(jnp.bfloat16)
    white = jnp.concatenate([white_ref[...], white_sib_ref[...]], axis=1)
    half = keep_ref.shape[0]
    send_ref[...] = nt_dot(lag_ref[half:, :], white).astype(jnp.bfloat16)
    keep_ref[...] = nt_dot(lag_ref[:half, :], white)


def add_kernel(keep_ref, recv_ref, kept_ref, send_ref):
    half = kept_ref.shape[0]
    kept_ref[...] = keep_ref[:half, :] + recv_ref[:half, :].astype(jnp.float32)
    send_ref[...] = (keep_ref[half:, :] + recv_ref[half:, :].astype(jnp.float32)).astype(jnp.bfloat16)


def last_kernel(*refs):
    out_ref = refs[-1]
    row = 0
    for keep_ref, recv_ref in zip(refs[:-1:2], refs[1:-1:2]):
        count = keep_ref.shape[0]
        out_ref[row : row + count, :] = keep_ref[...] + recv_ref[...].astype(jnp.float32)
        row += count


def local(raw_traces, fir_taps, sources, dead_flags):
    rows, samples = raw_traces.shape
    windows = samples // SPAN
    depth = windows * TD
    late = windows - 1
    time_parts = lax.axis_size("tm")
    chan_parts = lax.axis_size("chan")
    me = lax.axis_index("tm")
    per_dest = VS // time_parts
    bits = [1 << i for i in range(1, time_parts.bit_length() - 1)]
    scale = per_dest / sum(CHUNKS)
    sizes = [int(size * scale) for size in CHUNKS]

    history = lax.ppermute(
        raw_traces[:, samples - TAPS :], "tm", [(i, i + 1) for i in range(time_parts - 1)]
    )

    relative, offset = [], []
    begin = 0
    for size in sizes:
        for core in (0, 1):
            for code in range(time_parts // 2):
                rel = core
                for place, bit in enumerate(bits):
                    rel += bit * (code >> (len(bits) - 1 - place) & 1)
                relative += [rel] * size
                offset += list(range(begin, begin + size))
        begin += size
    wanted = per_dest * jnp.bitwise_xor(me, np.array(relative, np.int32)) + np.array(offset, np.int32)
    ordered = jnp.sum(jnp.where(wanted[:, None] == jnp.arange(VS)[None, :], sources[None, :], 0), axis=1)
    place = ordered - lax.axis_index("chan") * rows
    selector = (place[:, None] == jnp.arange(rows)[None, :]).astype(jnp.bfloat16)

    alive = jnp.broadcast_to((1 - dead_flags).astype(jnp.float32)[:, None], (rows, HALF))
    base = fir_base(fir_taps)
    table = jnp.asarray(dft_table())
    band = jnp.asarray(band_table())
    row_block = ROW_BLOCK if rows % ROW_BLOCK == 0 else rows
    fir_scratch = pltpu.VMEM((TD, SPAN + TAPS), jnp.bfloat16)
    fir_flops = 2 * rows * TD * (SPAN + TAPS + TD + HALF)

    late_white = pl.pallas_call(
        functools.partial(late_kernel, row_block),
        out_shape=jax.ShapeDtypeStruct((rows, late * TD), jnp.bfloat16),
        in_specs=[ANY] + [VMEM] * 4,
        out_specs=VMEM,
        scratch_shapes=[
            fir_scratch,
            pltpu.VMEM((rows, late * SPAN + TAPS), jnp.bfloat16),
            pltpu.SemaphoreType.DMA((late,)),
        ],
        compiler_params=params(),
        cost_estimate=cost(fir_flops * late, 2 * rows * samples),
        name="late_windows",
    )(raw_traces, base, table, band, alive)

    panel_shapes = []
    for size in sizes:
        panel_shapes += [jax.ShapeDtypeStruct((size * time_parts // 2, depth), jnp.bfloat16)] * 2
    *panels, white = pl.pallas_call(
        functools.partial(first_kernel, row_block, sizes),
        out_shape=panel_shapes + [jax.ShapeDtypeStruct((rows, depth), jnp.bfloat16)],
        in_specs=[ANY] + [VMEM] * 7,
        out_specs=[VMEM] * (len(panel_shapes) + 1),
        scratch_shapes=[fir_scratch, pltpu.VMEM((rows, SPAN), jnp.bfloat16), pltpu.SemaphoreType.DMA],
        compiler_params=params(),
        cost_estimate=cost(fir_flops + 2 * VS * rows * depth, 2 * (rows * SPAN + (rows + VS) * depth)),
        name="first_window",
    )(raw_traces, history, base, table, band, alive, late_white, selector)

    def across(panel):
        if chan_parts == 2:
            return swap(panel, "chan", 1)
        return lax.psum(panel, "chan") - panel

    cos_lag, sin_lag = (jnp.asarray(t) for t in lag_tables(1.0 / math.sqrt(time_parts * depth)))
    white_sib = None
    finals = []
    for q, size in enumerate(sizes):
        own, other = panels[2 * q : 2 * q + 2]
        own_in = across(own)
        sib = swap(other, "tm", 1)
        sib_in = across(sib)
        if white_sib is None:
            white_sib = swap(white, "tm", 1)
        count = own.shape[0]
        half = count * NLAG // 2
        keep, send = pl.pallas_call(
            main_kernel,
            out_shape=[
                jax.ShapeDtypeStruct((half, rows), jnp.float32),
                jax.ShapeDtypeStruct((half, rows), jnp.bfloat16),
            ],
            in_specs=[VMEM] * 8,
            out_specs=[VMEM] * 2,
            scratch_shapes=[pltpu.VMEM((count * NLAG, 2 * depth), jnp.bfloat16)],
            compiler_params=params(),
            cost_estimate=cost(2 * 2 * half * 2 * depth * rows, 4 * rows * depth + 6 * half * rows),
            name=f"product_{q}",
        )(own, own_in, sib, sib_in, white, white_sib, cos_lag, sin_lag)
        for bit in bits[:-1]:
            recv = swap(send, "tm", bit)
            half = keep.shape[0] // 2
            keep, send = pl.pallas_call(
                add_kernel,
                out_shape=[
                    jax.ShapeDtypeStruct((half, rows), jnp.float32),
                    jax.ShapeDtypeStruct((half, rows), jnp.bfloat16),
                ],
                in_specs=[VMEM] * 2,
                out_specs=[VMEM] * 2,
                compiler_params=params(),
                cost_estimate=cost(2 * half * rows, 18 * half * rows),
                name=f"add_{q}_{bit}",
            )(keep, recv)
        finals += [keep, swap(send, "tm", bits[-1])]
    stacked = pl.pallas_call(
        last_kernel,
        out_shape=jax.ShapeDtypeStruct((per_dest * NLAG, rows), jnp.float32),
        in_specs=[VMEM] * len(finals),
        out_specs=VMEM,
        compiler_params=params(),
        cost_estimate=cost(per_dest * NLAG * rows, 10 * per_dest * NLAG * rows),
        name="last_sum",
    )(*finals)
    return stacked.reshape(per_dest, NLAG, rows)


def solution(mesh):
    return jax.shard_map(
        local,
        mesh=mesh,
        in_specs=(P("chan", "tm"), P(), P(), P("chan")),
        out_specs=P("tm", None, "chan"),
        check_vma=False,
    )
```

```python
import functools
import math

import jax
import jax.numpy as jnp
import numpy as np
from jax import lax
from jax.experimental import pallas as pl
from jax.experimental.pallas import tpu as pltpu
from jax.sharding import PartitionSpec as P

VS = 512
TD = 256
HALF = TD // 2
NLAG = 8
HW = 32
TAPS = 128
DECIM = 4
SPAN = DECIM * TD
VMEM_LIMIT = 20 * 1024 * 1024
BLOCK = 320
CHUNKS = (2, 8, 8, 8, 6)
FIRST = (1, 1, 0, 1, 0)
SECOND = ((2,), (4,), (0, 1), (3,))
THIRD = ((2,), (0,), (3,), (1,))
PLAN = (
    ('split', 0, (), ()),
    ('merge', 0, (1, 2, 3, 4), ()),
    ('product', 0, (), ()),
    ('product', 1, (), (('y', 1),)),
    ('product', 2, (), (('y', 2), ('first', 0))),
    ('product', 3, (), (('y', 3),)),
    ('second', 2, (), (('first', 1),)),
    ('product', 4, (), (('y', 4),)),
    ('second', 0, (), (('first', 2),)),
    ('third', 0, (), (('second', 2),)),
    ('second', 3, (), (('first', 3),)),
    ('third', 1, (), (('second', 0),)),
    ('second', 1, (), (('first', 4),)),
    ('sum', 0, (), (('third', 0),)),
    ('third', 2, (), (('second', 3),)),
    ('sum', 1, (), (('third', 1),)),
    ('third', 3, (), (('second', 1),)),
    ('sum', 2, (), (('third', 2),)),
)
BASE_COST = 0.05
COSTS = {'split_0': 8, 'merge_0': 1, 'product_0': 0.265, 'product_1': 0.558, 'product_2': 0.604, 'product_3': 0.385, 'second_2': 0.186, 'product_4': 0.345, 'second_0': 0.23, 'third_0': 0.266, 'second_3': 0.245, 'third_1': 0.266, 'second_1': 0.186, 'sum_0': 0.047, 'third_2': 0.271, 'sum_1': 0.111, 'third_3': 0.368, 'sum_2': 0.293}

VMEM = pl.BlockSpec(memory_space=pltpu.VMEM)
ANY = pl.BlockSpec(memory_space=pl.ANY)


def params(limit=VMEM_LIMIT):
    return pltpu.CompilerParams(vmem_limit_bytes=limit)


def cost(flops, nbytes):
    return pl.CostEstimate(flops=int(flops), bytes_accessed=int(nbytes), transcendentals=0)


def swap(value, axis, bit):
    return lax.ppermute(value, axis, [(i, i ^ bit) for i in range(lax.axis_size(axis))])


def dft_table():
    phase = np.arange(TD)[:, None] * np.arange(HALF)[None, :] % TD
    angles = np.float32(2.0 * math.pi / TD) * phase.astype(np.float32)
    return np.concatenate([np.cos(angles), -np.sin(angles)], axis=1).astype(jnp.bfloat16)


def lag_tables(gain):
    phase = (np.arange(NLAG) - NLAG // 2)[:, None] * np.arange(HALF)[None, :] % TD
    angles = 2.0 * math.pi / TD * phase.astype(np.float64)
    return (gain * np.cos(angles)).astype(np.float32), (gain * np.sin(angles)).astype(np.float32)


def band_table():
    bins = np.arange(HALF)
    band = (np.abs(bins[:, None] - bins[None, :]) <= HW).astype(np.float32)
    return np.concatenate([band, band], axis=0).astype(jnp.bfloat16)


def nt_dot(left, right):
    return lax.dot_general(left, right, (((1,), (1,)), ((), ())), preferred_element_type=jnp.float32)


def history_kernel(raw_ref, out_ref, sem):
    samples = raw_ref.shape[1]
    copy = pltpu.make_async_copy(raw_ref.at[:, samples - TAPS :], out_ref, sem)
    copy.start()
    copy.wait()


def fill_fir(taps_ref, fir_ref):
    rows = TAPS // DECIM
    taps = jnp.broadcast_to(taps_ref[...].astype(jnp.float32), (rows, TAPS))
    padded = jnp.concatenate([taps, jnp.zeros_like(taps)], axis=1)
    base = pltpu.roll(padded, 1, 1, stride=DECIM, stride_axis=0).astype(jnp.bfloat16)
    fir_ref[...] = jnp.zeros_like(fir_ref)
    for i in range(TD // rows):
        fir_ref[rows * i : rows * (i + 1), TAPS * i : TAPS * (i + 2)] = base


def fill_alive(dead_ref, alive_ref):
    alive = 1.0 - dead_ref[...].astype(jnp.float32)
    for i in range(0, alive_ref.shape[0], HALF):
        alive_ref[i : i + HALF, :] = jnp.broadcast_to(alive[:, i : i + HALF], (HALF, HALF)).T


def fill_selector(sizes, orders, sources_ref, select_ref):
    rows = select_ref.shape[1]
    me = lax.axis_index("tm")
    first_chan = lax.axis_index("chan") * rows
    per_dest = sum(sizes)
    codes = 1 << len(orders[0])
    channels = sources_ref[...].astype(jnp.float32)
    begin, row = 0, 0
    for size, bits in zip(sizes, orders):
        count = 2 * codes * size
        index = lax.broadcasted_iota(jnp.int32, (count, VS), 0)
        scale = (1 << 16) // size + 1
        piece = lax.shift_right_logical(index * scale, 16)
        relative = lax.shift_right_logical(piece, len(bits))
        for place, bit in enumerate(bits):
            relative = relative + bit * (lax.shift_right_logical(piece, len(bits) - 1 - place) & 1)
        wanted = per_dest * jnp.bitwise_xor(relative, me) + begin + (index - size * piece)
        match = wanted == lax.broadcasted_iota(jnp.int32, (count, VS), 1)
        chosen = jnp.sum(jnp.where(match, channels, 0.0), axis=1, keepdims=True)
        place = chosen.astype(jnp.int32) - first_chan
        hit = place == lax.broadcasted_iota(jnp.int32, (count, rows), 1)
        select_ref[row : row + count, :] = jnp.where(hit, 1.0, 0.0).astype(jnp.bfloat16)
        begin += size
        row += count


def whiten(dec, table_ref, band_ref, alive):
    spectrum = jnp.dot(dec, table_ref[...], preferred_element_type=jnp.float32)
    real_part = spectrum[:, :HALF]
    imag_part = spectrum[:, HALF:]
    amplitude = jnp.sqrt(real_part * real_part + imag_part * imag_part)
    high = amplitude.astype(jnp.bfloat16)
    low = (amplitude - high.astype(jnp.float32)).astype(jnp.bfloat16)
    total = jnp.dot(
        jnp.concatenate([high, low], axis=1), band_ref[...], preferred_element_type=jnp.float32
    )
    factor = alive / (total * (1.0 / (2 * HW + 1)) + 1e-06)
    return jnp.concatenate([real_part * factor, imag_part * factor], axis=1).astype(jnp.bfloat16)


def late_kernel(
    sizes, orders, raw_ref, taps_ref, dead_ref, sources_ref, table_ref, band_ref,
    out_ref, fir_ref, alive_ref, select_ref,
):
    windows, rows, _ = out_ref.shape
    fill_fir(taps_ref, fir_ref)
    fill_alive(dead_ref, alive_ref)
    fill_selector(sizes, orders, sources_ref, select_ref)
    samples = jnp.concatenate(
        [raw_ref[:, w * SPAN - TAPS : (w + 1) * SPAN] for w in range(1, windows + 1)], axis=0
    )
    dec = nt_dot(samples, fir_ref[...]).astype(jnp.bfloat16)
    alive = jnp.concatenate([alive_ref[...]] * windows, axis=0)
    out_ref[...] = whiten(dec, table_ref, band_ref, alive).reshape(out_ref.shape)


def pick(select, white):
    return jnp.dot(select, white, preferred_element_type=jnp.float32).astype(jnp.bfloat16)


def first_kernel(
    raw_ref, hist_ref, fir_ref, table_ref, band_ref, alive_ref, late_ref, select_ref,
    panel_ref, white_ref,
):
    white_ref[1:] = late_ref[...]
    samples = jnp.concatenate([hist_ref[...], raw_ref[:, :SPAN]], axis=1)
    dec = nt_dot(samples, fir_ref[...]).astype(jnp.bfloat16)
    white_ref[0] = whiten(dec, table_ref, band_ref, alive_ref[...])
    select = select_ref[: panel_ref.shape[1]]
    for w in range(white_ref.shape[0]):
        panel_ref[w] = pick(select, white_ref[w])


def panels_kernel(skip, counts, select_ref, white_ref, own_ref, other_ref):
    for w in range(white_ref.shape[0]):
        chosen = pick(select_ref[skip:], white_ref[w])
        row, place = 0, 0
        for count in counts:
            own_ref[w, place : place + count] = chosen[row : row + count]
            other_ref[w, place : place + count] = chosen[row + count : row + 2 * count]
            row += 2 * count
            place += count


def merge_kernel(own_ref, sib_ref, *panel_refs):
    row = 0
    for panel_ref in panel_refs:
        count = panel_ref.shape[2]
        panel_ref[0] = own_ref[:, row : row + count]
        panel_ref[1] = sib_ref[:, row : row + count]
        row += count


def split_kernel(panel_ref, recv_ref, keep_ref, send_ref):
    count = keep_ref.shape[1]
    keep_ref[...] = panel_ref[:, :count] + recv_ref[:, :count]
    send_ref[...] = panel_ref[:, count:] + recv_ref[:, count:]


def product_kernel(sources, white_ref, white_sib_ref, cos_ref, sin_ref, keep_ref, send_ref, lag_ref):
    windows = white_ref.shape[0]
    half = keep_ref.shape[0]
    cos_lag = cos_ref[...][None]
    sin_lag = sin_ref[...][None]
    for side in range(2):
        for w in range(windows):
            source = sources(side, w)
            count = source.shape[0]
            real_src = source[:, None, :HALF]
            imag_src = source[:, None, HALF:]
            real_out = real_src * cos_lag + imag_src * sin_lag
            imag_out = imag_src * cos_lag - real_src * sin_lag
            k = (side * windows + w) * TD
            lag_ref[:, k : k + HALF] = real_out.reshape(count * NLAG, HALF).astype(jnp.bfloat16)
            lag_ref[:, k + HALF : k + TD] = imag_out.reshape(count * NLAG, HALF).astype(jnp.bfloat16)
    white = jnp.concatenate(
        [ref[w] for ref in (white_ref, white_sib_ref) for w in range(windows)], axis=1
    )
    blocks = -(-half // BLOCK)
    size = half // blocks
    for row in range(0, half, size):
        send_ref[row : row + size] = nt_dot(lag_ref[half + row : half + row + size], white).astype(jnp.bfloat16)
    for row in range(0, half, size):
        keep_ref[row : row + size] = nt_dot(lag_ref[row : row + size], white)


def taken_kernel(own_ref, sib_ref, *refs):
    product_kernel(lambda side, w: (own_ref, sib_ref)[side][w].astype(jnp.float32), *refs)


def summed_kernel(panel_ref, recv_ref, *refs):
    def sources(side, w):
        return panel_ref[side, w].astype(jnp.float32) + recv_ref[side, w].astype(jnp.float32)

    product_kernel(sources, *refs)


def halves_kernel(pieces, *refs):
    *parts, kept_ref, send_ref = refs
    place = 0
    for keep_ref, recv_ref, counts in zip(parts[::2], parts[1::2], pieces):
        row = 0
        for count in counts:
            half = count // 2
            for out_ref, begin in ((kept_ref, row), (send_ref, row + half)):
                rows = slice(begin, begin + half)
                value = keep_ref[rows, :] + recv_ref[rows, :].astype(jnp.float32)
                out_ref[place : place + half, :] = value.astype(out_ref.dtype)
            row += count
            place += half


def total_kernel(keep_ref, recv_ref, out_ref):
    out_ref[...] = keep_ref[...] + recv_ref[...].astype(jnp.float32)


def last_kernel(pieces, *refs):
    *parts, out_ref = refs
    parts = iter(parts)
    for summed, places in pieces:
        keep_ref = next(parts)
        recv_ref = None if summed else next(parts)
        row = 0
        for begin, count in places:
            rows = slice(row, row + count)
            value = keep_ref[rows, :]
            if not summed:
                value = value + recv_ref[rows, :].astype(jnp.float32)
            out_ref[begin : begin + count, :] = value
            row += count


class Chain:
    def __init__(self):
        self.last = None

    def __call__(self, name, kernel, args, outs, scratch=(), gates=(), waits=(), limit=VMEM_LIMIT, first=VMEM):
        args, gates = list(args), list(gates)
        order = [*waits] if self.last is None else [*waits, self.last]
        taken, passed = len(args), len(args) + len(gates) + len(order)

        def body(*refs):
            written = refs[passed : passed + len(outs)]
            kernel(*refs[:taken], *written, *refs[passed + len(outs) + len(gates) :])

        results = pl.pallas_call(
            body,
            out_shape=[*outs, *(jax.ShapeDtypeStruct(g.shape, g.dtype) for g in gates)],
            in_specs=[first] + [VMEM] * (taken - 1) + [ANY] * (len(gates) + len(order)),
            out_specs=[VMEM] * len(outs) + [ANY] * len(gates),
            input_output_aliases={taken + i: len(outs) + i for i in range(len(gates))},
            scratch_shapes=list(scratch),
            compiler_params=params(limit),
            cost_estimate=cost(1e9 * COSTS.get(name, BASE_COST), 1e4),
            name=name,
        )(*args, *gates, *order)
        self.last = results[0]
        return results


def local(raw_traces, fir_taps, sources, dead_flags):
    rows, samples = raw_traces.shape
    windows = samples // SPAN
    late = windows - 1
    time_parts = lax.axis_size("tm")
    chan_parts = lax.axis_size("chan")
    per_dest = VS // time_parts
    codes = time_parts // 2
    bits = [1 << i for i in range(1, time_parts.bit_length() - 1)]
    sizes, firsts, seconds, thirds, plan = CHUNKS, FIRST, SECOND, THIRD, PLAN
    if per_dest != sum(CHUNKS) or len(bits) != 3:
        sizes, firsts = (per_dest // 2,) * 2, (0, 0)
        seconds = thirds = ((0,), (1,))
        plan = [("split", 0, (), ()), ("merge", 0, (), ()), ("product", 0, (1,), ()), ("product", 1, (), ())]
        final = "third" + "+" * (len(bits) - 3)
        plan += [(name, q, (), ()) for name in ("second", *(final[:5 + i] for i in range(len(final) - 4))) for q in (0, 1)]
    final = "third" + "+" * (len(bits) - 3)
    orders = [[bits[first], *bits[:first], *bits[first + 1 :]] for first in firsts]
    counts = [size * codes for size in sizes]
    bf16, f32 = jnp.bfloat16, jnp.float32
    shape = jax.ShapeDtypeStruct
    chain = Chain()

    (tail,) = chain(
        "history", history_kernel, [pltpu.with_memory_space_constraint(raw_traces, pltpu.HBM)], [shape((rows, TAPS), bf16)], [pltpu.SemaphoreType.DMA],
        first=ANY,
    )
    history = lax.ppermute(tail, "tm", [(i, i + 1) for i in range(time_parts - 1)])

    table = jnp.asarray(dft_table())
    band = jnp.asarray(band_table())
    late_white, fir, alive, select = chain(
        "late",
        functools.partial(late_kernel, sizes, orders),
        [raw_traces, fir_taps.reshape(1, -1), dead_flags.reshape(1, -1), sources.reshape(1, -1), table, band],
        [
            shape((late, rows, TD), bf16),
            shape((TD, SPAN + TAPS), bf16),
            shape((rows, HALF), f32),
            shape((VS, rows), bf16),
        ],
    )
    panel, white = chain(
        "first",
        first_kernel,
        [raw_traces, history, fir, table, band, alive, late_white, select],
        [shape((windows, 2 * counts[0], TD), bf16), shape((windows, rows, TD), bf16)],
    )
    rest = shape((windows, sum(counts[1:]), TD), bf16)
    own, other = chain(
        "panels", functools.partial(panels_kernel, 2 * counts[0], counts[1:]), [select, white], [rest, rest]
    )
    white_sib = swap(white, "tm", 1)
    sib = swap(other, "tm", 1)
    tables = [jnp.asarray(t) for t in lag_tables(1.0 / math.sqrt(time_parts * windows * TD))]
    spectra = [white, white_sib, *tables]

    def across(panel):
        if chan_parts == 2:
            return swap(panel, "chan", 1)
        return lax.psum(panel, "chan") - panel

    panels = {0: panel}
    arrived = {}
    state, pieces, moved = {}, {}, {}
    for kind, q, leaving, waits in plan:
        name = f"{kind}_{q}"
        gates = [panels[g] for g in leaving if g in panels]
        held = [moved[key] for key in waits if key in moved]
        call = functools.partial(chain, name, gates=gates, waits=held)
        if kind == "split":
            half = shape((windows, counts[0], TD), bf16)
            keep, send, *let = call(split_kernel, [panel, across(panel)], [half, half])
            taken = [keep, swap(send, "tm", 1)]
        elif kind == "merge":
            made = call(merge_kernel, [own, sib], [shape((2, windows, c, TD), bf16) for c in counts[1:]])
            panels.update(enumerate(made, 1))
            let = []
        elif kind == "product":
            half = counts[q] * NLAG // 2
            args = taken if q == 0 else [panels[q], arrived[q]]
            keep, send, *let = call(
                summed_kernel if q else taken_kernel, [*args, *spectra],
                [shape((half, rows), f32), shape((half, rows), bf16)],
                [pltpu.VMEM((2 * half, 2 * windows * TD), bf16)],
            )
            moved["first", q] = swap(send, "tm", orders[q][0])
            state["first", q] = keep, moved["first", q]
            pieces["first", q] = [half]
        elif kind == "sum":
            keep, recv = state["third", q]
            total, *let = call(total_kernel, [keep, recv], [shape(keep.shape, f32)])
            state["third", q] = total, None
        else:
            before, groups = {"second": ("first", seconds), "third": ("second", thirds)}.get(kind, (kind[:-1], thirds))
            members = [(before, member) for member in groups[q]]
            if before.startswith("third"):
                members = [(before, q)]
            split = [pieces[m] for m in members]
            half = sum(map(sum, split)) // 2
            keep, send, *let = call(
                functools.partial(halves_kernel, split), [x for m in members for x in state[m]],
                [shape((half, rows), f32), shape((half, rows), bf16)],
            )
            pieces[kind, q] = [count // 2 for part in split for count in part]
            chunk = groups[q][0] if kind == "second" else seconds[groups[q][0]][0]
            stage = 1 if kind == "second" else 2 + kind.count("+")
            moved[kind, q] = swap(send, "tm", orders[chunk][stage])
            state[kind, q] = keep, moved[kind, q]
        panels.update(zip(leaving, let))
        for g in leaving:
            moved["y", g] = arrived[g] = across(panels[g])

    starts = [sum(sizes[:q]) * NLAG for q in range(len(sizes))]
    args, places = [], []
    for q, group in enumerate(thirds):
        args += [x for x in state[final, q] if x is not None]
        chunks = [chunk for member in group for chunk in seconds[member]]
        places.append((state[final, q][1] is None, [(starts[chunk], sizes[chunk] * NLAG) for chunk in chunks]))
    (stacked,) = chain(
        "last", functools.partial(last_kernel, places), args, [shape((per_dest * NLAG, rows), f32)]
    )
    return stacked.reshape(per_dest, NLAG, rows)


def solution(mesh):
    return jax.shard_map(
        local,
        mesh=mesh,
        in_specs=(P("chan", "tm"), P(), P(), P("chan")),
        out_specs=P("tm", None, "chan"),
        check_vma=False,
    )
```

```python
import functools
import math

import jax
import jax.numpy as jnp
import numpy as np
from jax import lax
from jax.experimental import pallas as pl
from jax.experimental.pallas import tpu as pltpu
from jax.sharding import PartitionSpec as P

VS = 512
TD = 256
HALF = TD // 2
NLAG = 8
HW = 32
TAPS = 128
DECIM = 4
SPAN = DECIM * TD
VMEM_LIMIT = 20 * 1024 * 1024
CHUNKS = (10, 8, 8, 6)
FIRST = (1, 0, 1, 0)
SECOND = ((1,), (3,), (0,), (2,))
THIRD = ((2,), (0,), (3,), (1,))
ACROSS = ((1,), (2,), (3,))
PLAN = (
    ('merge', 0, (1, 2, 3), ()),
    ('split', 0, (), ()),
    ('send', 0, (), ()),
    ('keep', 0, (), ()),
    ('send', 1, (), (('y', 1),)),
    ('keep', 1, (), ()),
    ('send', 2, (), (('y', 2),)),
    ('keep', 2, (), ()),
    ('second', 2, (), (('first', 0),)),
    ('send', 3, (), (('y', 3), ('first', 1))),
    ('second', 0, (), ()),
    ('keep', 3, (), ()),
    ('third', 0, (), ()),
    ('second', 3, (), (('first', 2), ('second', 2))),
    ('third', 1, (), (('second', 0),)),
    ('second', 1, (), (('first', 3),)),
    ('sum', 0, (), (('third', 0),)),
    ('third', 2, (), (('second', 3),)),
    ('sum', 1, (), (('third', 1),)),
    ('third', 3, (), (('second', 1),)),
    ('sum', 2, (), (('third', 2),)),
)
BASE_COST = 0.05
COSTS = {
    'merge_0': 0.52,
    'split_0': 0.165,
    'send_0': 0.297,
    'keep_0': 0.182,
    'send_1': 15,
    'keep_1': 0.347,
    'send_2': 0.277,
    'second_2': 0.191,
    'keep_2': 0.112,
    'send_3': 0.275,
    'second_0': 0.191,
    'keep_3': 0.11,
    'third_0': 0.286,
    'second_3': 0.191,
    'third_1': 0.286,
    'second_1': 4,
    'sum_0': 0.027,
    'third_2': 0.304,
    'sum_1': 1,
    'third_3': 0.373,
    'sum_2': 0.293,
    'panels': 0.5,
    'gate': 0.05,
    'first': 0.5,
}

VMEM = pl.BlockSpec(memory_space=pltpu.VMEM)
ANY = pl.BlockSpec(memory_space=pl.ANY)


def params(limit=VMEM_LIMIT):
    return pltpu.CompilerParams(vmem_limit_bytes=limit)


def cost(flops, nbytes):
    return pl.CostEstimate(flops=int(flops), bytes_accessed=int(nbytes), transcendentals=0)


def swap(value, axis, bit):
    return lax.ppermute(value, axis, [(i, i ^ bit) for i in range(lax.axis_size(axis))])


def dft_table():
    phase = np.arange(TD)[:, None] * np.arange(HALF)[None, :] % TD
    angles = np.float32(2.0 * math.pi / TD) * phase.astype(np.float32)
    return np.concatenate([np.cos(angles), -np.sin(angles)], axis=1).astype(jnp.bfloat16)


def lag_tables(gain):
    phase = (np.arange(NLAG) - NLAG // 2)[:, None] * np.arange(HALF)[None, :] % TD
    angles = 2.0 * math.pi / TD * phase.astype(np.float64)
    return (gain * np.cos(angles)).astype(np.float32), (gain * np.sin(angles)).astype(np.float32)


def band_table():
    bins = np.arange(HALF)
    band = (np.abs(bins[:, None] - bins[None, :]) <= HW).astype(np.float32)
    return np.concatenate([band, band], axis=0).astype(jnp.bfloat16)


def nt_dot(left, right):
    return lax.dot_general(left, right, (((1,), (1,)), ((), ())), preferred_element_type=jnp.float32)


def history_kernel(raw_ref, out_ref, sem):
    samples = raw_ref.shape[1]
    copy = pltpu.make_async_copy(raw_ref.at[:, samples - TAPS :], out_ref, sem)
    copy.start()
    copy.wait()


def fill_fir(taps_ref, fir_ref):
    rows = TAPS // DECIM
    taps = jnp.broadcast_to(taps_ref[...].astype(jnp.float32), (rows, TAPS))
    padded = jnp.concatenate([taps, jnp.zeros_like(taps)], axis=1)
    base = pltpu.roll(padded, 1, 1, stride=DECIM, stride_axis=0).astype(jnp.bfloat16)
    fir_ref[...] = jnp.zeros_like(fir_ref)
    for i in range(TD // rows):
        fir_ref[rows * i : rows * (i + 1), TAPS * i : TAPS * (i + 2)] = base


def fill_alive(dead_ref, alive_ref):
    alive = 1.0 - dead_ref[...].astype(jnp.float32)
    for i in range(0, alive_ref.shape[0], HALF):
        alive_ref[i : i + HALF, :] = jnp.broadcast_to(alive[:, i : i + HALF], (HALF, HALF)).T


def fill_selector(sizes, orders, sources_ref, select_ref):
    rows = select_ref.shape[1]
    me = lax.axis_index("tm")
    first_chan = lax.axis_index("chan") * rows
    per_dest = sum(sizes)
    codes = 1 << len(orders[0])
    channels = sources_ref[...].astype(jnp.float32)
    begin, row = 0, 0
    for size, bits in zip(sizes, orders):
        count = 2 * codes * size
        index = lax.broadcasted_iota(jnp.int32, (count, VS), 0)
        scale = (1 << 16) // size + 1
        piece = lax.shift_right_logical(index * scale, 16)
        relative = lax.shift_right_logical(piece, len(bits))
        for place, bit in enumerate(bits):
            relative = relative + bit * (lax.shift_right_logical(piece, len(bits) - 1 - place) & 1)
        wanted = per_dest * jnp.bitwise_xor(relative, me) + begin + (index - size * piece)
        match = wanted == lax.broadcasted_iota(jnp.int32, (count, VS), 1)
        chosen = jnp.sum(jnp.where(match, channels, 0.0), axis=1, keepdims=True)
        place = chosen.astype(jnp.int32) - first_chan
        hit = place == lax.broadcasted_iota(jnp.int32, (count, rows), 1)
        select_ref[row : row + count, :] = jnp.where(hit, 1.0, 0.0).astype(jnp.bfloat16)
        begin += size
        row += count


def whiten(dec, table_ref, band_ref, alive):
    spectrum = jnp.dot(dec, table_ref[...], preferred_element_type=jnp.float32)
    real_part = spectrum[:, :HALF]
    imag_part = spectrum[:, HALF:]
    amplitude = jnp.sqrt(real_part * real_part + imag_part * imag_part)
    high = amplitude.astype(jnp.bfloat16)
    low = (amplitude - high.astype(jnp.float32)).astype(jnp.bfloat16)
    total = jnp.dot(
        jnp.concatenate([high, low], axis=1), band_ref[...], preferred_element_type=jnp.float32
    )
    factor = alive / (total * (1.0 / (2 * HW + 1)) + 1e-06)
    return jnp.concatenate([real_part * factor, imag_part * factor], axis=1).astype(jnp.bfloat16)


def late_kernel(
    sizes, orders, raw_ref, taps_ref, dead_ref, sources_ref, table_ref, band_ref,
    out_ref, fir_ref, alive_ref, select_ref,
):
    windows, rows, _ = out_ref.shape
    fill_fir(taps_ref, fir_ref)
    fill_alive(dead_ref, alive_ref)
    fill_selector(sizes, orders, sources_ref, select_ref)
    samples = jnp.concatenate(
        [raw_ref[:, w * SPAN - TAPS : (w + 1) * SPAN] for w in range(1, windows + 1)], axis=0
    )
    dec = nt_dot(samples, fir_ref[...]).astype(jnp.bfloat16)
    alive = jnp.concatenate([alive_ref[...]] * windows, axis=0)
    out_ref[...] = whiten(dec, table_ref, band_ref, alive).reshape(out_ref.shape)


def pick(select, white):
    return jnp.dot(select, white, preferred_element_type=jnp.float32).astype(jnp.bfloat16)


def first_kernel(
    raw_ref, hist_ref, fir_ref, table_ref, band_ref, alive_ref, late_ref, select_ref,
    panel_ref, white_ref,
):
    white_ref[1:] = late_ref[...]
    samples = jnp.concatenate([hist_ref[...], raw_ref[:, :SPAN]], axis=1)
    dec = nt_dot(samples, fir_ref[...]).astype(jnp.bfloat16)
    white_ref[0] = whiten(dec, table_ref, band_ref, alive_ref[...])
    select = select_ref[: panel_ref.shape[1]]
    for w in range(white_ref.shape[0]):
        panel_ref[w] = pick(select, white_ref[w])


def panels_kernel(skip, groups, select_ref, white_ref, *refs):
    own_refs, other_refs = refs[: len(groups)], refs[len(groups) :]
    for w in range(white_ref.shape[0]):
        chosen = pick(select_ref[skip:], white_ref[w])
        row = 0
        for group, own_ref, other_ref in zip(groups, own_refs, other_refs):
            place = 0
            for count in group:
                own_ref[w, place : place + count] = chosen[row : row + count]
                other_ref[w, place : place + count] = chosen[row + count : row + 2 * count]
                row += 2 * count
                place += count


def merge_kernel(*refs):
    groups = len(refs) // 3
    for own_ref, sib_ref, panel_ref in zip(refs[:groups], refs[groups : 2 * groups], refs[2 * groups :]):
        panel_ref[0] = own_ref[...]
        panel_ref[1] = sib_ref[...]


def gate_kernel(table_ref, out_ref):
    out_ref[...] = jnp.zeros_like(out_ref)


def split_kernel(panel_ref, recv_ref, keep_ref, send_ref):
    count = keep_ref.shape[1]
    keep_ref[...] = panel_ref[:, :count] + recv_ref[:, :count]
    send_ref[...] = panel_ref[:, count:] + recv_ref[:, count:]


def product_kernel(sources, begin, white_ref, white_sib_ref, cos_ref, sin_ref, out_ref):
    windows = white_ref.shape[0]
    count = out_ref.shape[0]
    cos_lag = cos_ref[...][None]
    sin_lag = sin_ref[...][None]
    white = jnp.concatenate(
        [ref[w] for ref in (white_ref, white_sib_ref) for w in range(windows)], axis=1
    )
    parts = []
    for side in range(2):
        for w in range(windows):
            source = sources(side, w, begin // NLAG, count // NLAG)
            real_src = source[:, None, :HALF]
            imag_src = source[:, None, HALF:]
            for part in (
                real_src * cos_lag + imag_src * sin_lag,
                imag_src * cos_lag - real_src * sin_lag,
            ):
                parts.append(part.reshape(count, HALF).astype(jnp.bfloat16))
    out_ref[...] = nt_dot(jnp.concatenate(parts, axis=1), white).astype(out_ref.dtype)


def taken_kernel(first, own_ref, sib_ref, *refs):
    def sources(side, w, begin, count):
        return (own_ref, sib_ref)[side][w, begin : begin + count].astype(jnp.float32)

    product_kernel(sources, first, *refs)


def summed_kernel(place, first, panel_ref, recv_ref, *refs):
    def sources(side, w, begin, count):
        rows = slice(place + begin, place + begin + count)
        return panel_ref[side, w, rows].astype(jnp.float32) + recv_ref[side, w, rows].astype(jnp.float32)

    product_kernel(sources, first, *refs)


def halves_kernel(pieces, *refs):
    *parts, kept_ref, send_ref = refs
    place = 0
    for keep_ref, recv_ref, counts in zip(parts[::2], parts[1::2], pieces):
        row = 0
        for count in counts:
            half = count // 2
            for out_ref, begin in ((kept_ref, row), (send_ref, row + half)):
                rows = slice(begin, begin + half)
                value = keep_ref[rows, :] + recv_ref[rows, :].astype(jnp.float32)
                out_ref[place : place + half, :] = value.astype(out_ref.dtype)
            row += count
            place += half


def total_kernel(keep_ref, recv_ref, out_ref):
    out_ref[...] = keep_ref[...] + recv_ref[...].astype(jnp.float32)


def last_kernel(pieces, *refs):
    *parts, out_ref, late_ref, sems = refs
    parts = iter(parts)
    copies, place = [], 0
    for summed, places in sorted(pieces, key=lambda piece: not piece[0]):
        keep_ref = next(parts)
        recv_ref = None if summed else next(parts)
        row = 0
        for begin, count in places:
            source = keep_ref.at[row : row + count]
            if not summed:
                rows = slice(row, row + count)
                late_ref[place : place + count] = keep_ref[rows, :] + recv_ref[rows, :].astype(jnp.float32)
                source = late_ref.at[place : place + count]
                place += count
            copy = pltpu.make_async_copy(source, out_ref.at[begin : begin + count], sems.at[len(copies)])
            copy.start()
            copies.append(copy)
            row += count
    for copy in copies:
        copy.wait()


class Chain:
    def __init__(self):
        self.last = None

    def __call__(self, name, kernel, args, outs, scratch=(), gates=(), waits=(), limit=VMEM_LIMIT, first=VMEM, result=VMEM):
        args, gates = list(args), list(gates)
        order = [*waits] if self.last is None else [*waits, self.last]
        taken, passed = len(args), len(args) + len(gates) + len(order)

        def body(*refs):
            written = refs[passed : passed + len(outs)]
            kernel(*refs[:taken], *written, *refs[passed + len(outs) + len(gates) :])

        results = pl.pallas_call(
            body,
            out_shape=[*outs, *(jax.ShapeDtypeStruct(g.shape, g.dtype) for g in gates)],
            in_specs=[first] + [VMEM] * (taken - 1) + [ANY] * (len(gates) + len(order)),
            out_specs=[result] * len(outs) + [ANY] * len(gates),
            input_output_aliases={taken + i: len(outs) + i for i in range(len(gates))},
            scratch_shapes=list(scratch),
            compiler_params=params(limit),
            cost_estimate=cost(1e9 * COSTS.get(name, BASE_COST), 1e4),
            name=name,
        )(*args, *gates, *order)
        self.last = results[0]
        return results


def local(raw_traces, fir_taps, sources, dead_flags):
    rows, samples = raw_traces.shape
    windows = samples // SPAN
    late = windows - 1
    time_parts = lax.axis_size("tm")
    chan_parts = lax.axis_size("chan")
    per_dest = VS // time_parts
    codes = time_parts // 2
    bits = [1 << i for i in range(1, time_parts.bit_length() - 1)]
    sizes, firsts, seconds, thirds, plan = CHUNKS, FIRST, SECOND, THIRD, PLAN
    across_groups = ACROSS
    if per_dest != sum(CHUNKS) or len(bits) != 3:
        sizes, firsts = (per_dest // 2,) * 2, (0, 0)
        seconds = thirds = ((0,), (1,))
        across_groups = ((1,),)
        plan = [("split", 0, (), ()), ("merge", 0, (1,), ())]
        plan += [(kind, q, (), ()) for q in (0, 1) for kind in ("send", "keep")]
        final = "third" + "+" * (len(bits) - 3)
        plan += [(name, q, (), ()) for name in ("second", *(final[:5 + i] for i in range(len(final) - 4))) for q in (0, 1)]
    final = "third" + "+" * (len(bits) - 3)
    orders = [[bits[first], *bits[:first], *bits[first + 1 :]] for first in firsts]
    counts = [size * codes for size in sizes]
    bf16, f32 = jnp.bfloat16, jnp.float32
    shape = jax.ShapeDtypeStruct
    chain = Chain()

    (tail,) = chain(
        "history", history_kernel, [pltpu.with_memory_space_constraint(raw_traces, pltpu.HBM)], [shape((rows, TAPS), bf16)], [pltpu.SemaphoreType.DMA],
        first=ANY,
    )
    history = lax.ppermute(tail, "tm", [(i, i + 1) for i in range(time_parts - 1)])

    table = jnp.asarray(dft_table())
    band = jnp.asarray(band_table())
    late_white, fir, alive, select = chain(
        "late",
        functools.partial(late_kernel, sizes, orders),
        [raw_traces, fir_taps.reshape(1, -1), dead_flags.reshape(1, -1), sources.reshape(1, -1), table, band],
        [
            shape((late, rows, TD), bf16),
            shape((TD, SPAN + TAPS), bf16),
            shape((rows, HALF), f32),
            shape((VS, rows), bf16),
        ],
    )
    panel, white = chain(
        "first",
        first_kernel,
        [raw_traces, history, fir, table, band, alive, late_white, select],
        [shape((windows, 2 * counts[0], TD), bf16), shape((windows, rows, TD), bf16)],
    )
    members = [[counts[chunk] for chunk in group] for group in across_groups]
    rest = [shape((windows, sum(group), TD), bf16) for group in members]
    parts = chain("panels", functools.partial(panels_kernel, 2 * counts[0], members), [select, white], rest + rest)
    own, sib = parts[: len(rest)], [swap(other, "tm", 1) for other in parts[len(rest) :]]
    _, white = chain("gate", gate_kernel, [table], [shape((8, HALF), f32)], gates=[white])
    white_sib = swap(white, "tm", 1)
    tables = [jnp.asarray(t) for t in lag_tables(1.0 / math.sqrt(time_parts * windows * TD))]
    spectra = [white, white_sib, *tables]

    def across(panel):
        if chan_parts == 2:
            return swap(panel, "chan", 1)
        return lax.psum(panel, "chan") - panel

    panels = {0: panel}
    arrived = {}
    state, pieces, moved = {}, {}, {}
    for kind, q, leaving, waits in plan:
        name = f"{kind}_{q}"
        gates = [panels[g] for g in leaving if g in panels]
        held = [moved[key] for key in waits if key in moved]
        call = functools.partial(chain, name, gates=gates, waits=held)
        if kind == "split":
            half = shape((windows, counts[0], TD), bf16)
            keep, send, *let = call(split_kernel, [panel, across(panel)], [half, half])
            taken = [keep, swap(send, "tm", 1)]
        elif kind == "merge":
            totals = [sum(counts[chunk] for chunk in group) for group in across_groups]
            made = call(merge_kernel, [*own, *sib], [shape((2, windows, total, TD), bf16) for total in totals])
            panels.update(enumerate(made, 1))
            let = []
        elif kind in ("send", "keep"):
            half = counts[q] * NLAG // 2
            args, kernel = taken, taken_kernel
            for g, group in enumerate(across_groups, 1):
                if q in group:
                    place = sum(counts[chunk] for chunk in group if chunk < q)
                    args, kernel = [panels[g], arrived[g]], functools.partial(summed_kernel, place)
            made, *let = call(
                functools.partial(kernel, half if kind == "send" else 0), [*args, *spectra],
                [shape((half, rows), bf16 if kind == "send" else f32)],
            )
            if kind == "send":
                moved["first", q] = swap(made, "tm", orders[q][0])
                pieces["first", q] = [half]
            else:
                state["first", q] = made, moved["first", q]
        elif kind == "sum":
            keep, recv = state["third", q]
            total, *let = call(total_kernel, [keep, recv], [shape(keep.shape, f32)])
            state["third", q] = total, None
        else:
            before, groups = {"second": ("first", seconds), "third": ("second", thirds)}.get(kind, (kind[:-1], thirds))
            members = [(before, member) for member in groups[q]]
            if before.startswith("third"):
                members = [(before, q)]
            split = [pieces[m] for m in members]
            half = sum(map(sum, split)) // 2
            keep, send, *let = call(
                functools.partial(halves_kernel, split), [x for m in members for x in state[m]],
                [shape((half, rows), f32), shape((half, rows), bf16)],
            )
            pieces[kind, q] = [count // 2 for part in split for count in part]
            chunk = groups[q][0] if kind == "second" else seconds[groups[q][0]][0]
            stage = 1 if kind == "second" else 2 + kind.count("+")
            moved[kind, q] = swap(send, "tm", orders[chunk][stage])
            state[kind, q] = keep, moved[kind, q]
        panels.update(zip(leaving, let))
        for g in leaving:
            moved["y", g] = arrived[g] = across(panels[g])

    starts = [sum(sizes[:q]) * NLAG for q in range(len(sizes))]
    args, places = [], []
    for q, group in sorted(enumerate(thirds), key=lambda item: state[final, item[0]][1] is not None):
        args += [x for x in state[final, q] if x is not None]
        chunks = [chunk for member in group for chunk in seconds[member]]
        places.append((state[final, q][1] is None, [(starts[chunk], sizes[chunk] * NLAG) for chunk in chunks]))
    (stacked,) = chain(
        "last",
        functools.partial(last_kernel, places),
        args,
        [shape((per_dest * NLAG, rows), f32)],
        [pltpu.VMEM((per_dest * NLAG, rows), f32), pltpu.SemaphoreType.DMA((len(sizes),))],
        result=ANY,
    )
    return stacked.reshape(per_dest, NLAG, rows)


def solution(mesh):
    return jax.shard_map(
        local,
        mesh=mesh,
        in_specs=(P("chan", "tm"), P(), P(), P("chan")),
        out_specs=P("tm", None, "chan"),
        check_vma=False,
    )
```

```python
import functools
import math

import jax
import jax.numpy as jnp
import numpy as np
from jax import lax
from jax.experimental import pallas as pl
from jax.experimental.pallas import tpu as pltpu
from jax.sharding import PartitionSpec as P

VS = 512
TD = 256
HALF = TD // 2
NLAG = 8
HW = 32
TAPS = 128
DECIM = 4
SPAN = DECIM * TD
VMEM_LIMIT = 20 * 1024 * 1024
CHUNKS = (10, 8, 8, 6)
FIRST = (1, 0, 1, 0)
SECOND = ((1,), (3,), (0,), (2,))
THIRD = ((2,), (0,), (3,), (1,))
ACROSS = ((1,), (2,), (3,))
PLAN = (
    ('merge', 0, (1, 2), ()),
    ('split', 0, (3,), ()),
    ('send', 0, (), ()),
    ('keep', 0, (), ()),
    ('send', 1, (), (('y', 1),)),
    ('keep', 1, (), ()),
    ('send', 2, (), (('y', 2),)),
    ('second', 2, (), (('first', 0),)),
    ('keep', 2, (), ()),
    ('send', 3, (), (('y', 3), ('first', 1))),
    ('second', 0, (), ()),
    ('third', 0, (), ()),
    ('second', 3, (), (('first', 2),)),
    ('keep', 3, (), ()),
    ('third', 1, (), (('second', 0),)),
    ('second', 1, (), (('first', 3), ('second', 2))),
    ('sum', 0, (), (('third', 0),)),
    ('third', 2, (), (('second', 3),)),
    ('sum', 1, (), (('third', 1),)),
    ('third', 3, (), (('second', 1),)),
    ('sum', 2, (), ()),
)
BASE_COST = 0.05
COSTS = {
    'merge_0': 0.52,
    'split_0': 15,
    'send_0': 0.5,
    'keep_0': 0.182,
    'send_1': 15,
    'keep_1': 0.347,
    'send_2': 0.277,
    'second_2': 0.191,
    'keep_2': 0.112,
    'send_3': 0.275,
    'second_0': 0.191,
    'keep_3': 0.11,
    'third_0': 0.286,
    'second_3': 0.191,
    'third_1': 0.286,
    'second_1': 4,
    'sum_0': 0.027,
    'third_2': 0.304,
    'sum_1': 1,
    'third_3': 0.373,
    'sum_2': 0.293,
    'panels': 0.05,
    'gate': 0.05,
    'first': 0.5,
}

VMEM = pl.BlockSpec(memory_space=pltpu.VMEM)
ANY = pl.BlockSpec(memory_space=pl.ANY)


def params(limit=VMEM_LIMIT):
    return pltpu.CompilerParams(vmem_limit_bytes=limit)


def cost(flops, nbytes):
    return pl.CostEstimate(flops=int(flops), bytes_accessed=int(nbytes), transcendentals=0)


def swap(value, axis, bit):
    return lax.ppermute(value, axis, [(i, i ^ bit) for i in range(lax.axis_size(axis))])


def dft_table():
    phase = np.arange(TD)[:, None] * np.arange(HALF)[None, :] % TD
    angles = np.float32(2.0 * math.pi / TD) * phase.astype(np.float32)
    return np.concatenate([np.cos(angles), -np.sin(angles)], axis=1).astype(jnp.bfloat16)


def lag_tables(gain):
    phase = (np.arange(NLAG) - NLAG // 2)[:, None] * np.arange(HALF)[None, :] % TD
    angles = 2.0 * math.pi / TD * phase.astype(np.float64)
    return (gain * np.cos(angles)).astype(np.float32), (gain * np.sin(angles)).astype(np.float32)


def nt_dot(left, right):
    return lax.dot_general(left, right, (((1,), (1,)), ((), ())), preferred_element_type=jnp.float32)


def history_kernel(raw_ref, out_ref, sem):
    samples = raw_ref.shape[1]
    copy = pltpu.make_async_copy(raw_ref.at[:, samples - TAPS :], out_ref, sem)
    copy.start()
    copy.wait()


def fill_fir(taps_ref, fir_ref):
    rows = TAPS // DECIM
    taps = jnp.broadcast_to(taps_ref[...].astype(jnp.float32), (rows, TAPS))
    padded = jnp.concatenate([taps, jnp.zeros_like(taps)], axis=1)
    base = pltpu.roll(padded, 1, 1, stride=DECIM, stride_axis=0).astype(jnp.bfloat16)
    fir_ref[...] = jnp.zeros_like(fir_ref)
    for i in range(TD // rows):
        fir_ref[rows * i : rows * (i + 1), TAPS * i : TAPS * (i + 2)] = base


def fill_alive(dead_ref, alive_ref):
    alive = 1.0 - dead_ref[...].astype(jnp.float32)
    for i in range(0, alive_ref.shape[0], HALF):
        alive_ref[i : i + HALF, :] = jnp.broadcast_to(alive[:, i : i + HALF], (HALF, HALF)).T


def fill_band(band_ref):
    bins = lax.broadcasted_iota(jnp.int32, band_ref.shape, 0) & (HALF - 1)
    apart = jnp.abs(bins - lax.broadcasted_iota(jnp.int32, band_ref.shape, 1))
    band_ref[...] = jnp.where(apart <= HW, 1.0, 0.0).astype(jnp.bfloat16)


def fill_selector(sizes, orders, sources_ref, select_ref):
    rows = select_ref.shape[1]
    me = lax.axis_index("tm")
    first_chan = lax.axis_index("chan") * rows
    per_dest = sum(sizes)
    codes = 1 << len(orders[0])
    channels = sources_ref[...].astype(jnp.float32)
    begin, row = 0, 0
    for size, bits in zip(sizes, orders):
        count = 2 * codes * size
        index = lax.broadcasted_iota(jnp.int32, (count, VS), 0)
        scale = (1 << 16) // size + 1
        piece = lax.shift_right_logical(index * scale, 16)
        relative = lax.shift_right_logical(piece, len(bits))
        for place, bit in enumerate(bits):
            relative = relative + bit * (lax.shift_right_logical(piece, len(bits) - 1 - place) & 1)
        wanted = per_dest * jnp.bitwise_xor(relative, me) + begin + (index - size * piece)
        match = wanted == lax.broadcasted_iota(jnp.int32, (count, VS), 1)
        chosen = jnp.sum(jnp.where(match, channels, 0.0), axis=1, keepdims=True)
        place = chosen.astype(jnp.int32) - first_chan
        hit = place == lax.broadcasted_iota(jnp.int32, (count, rows), 1)
        select_ref[row : row + count, :] = jnp.where(hit, 1.0, 0.0).astype(jnp.bfloat16)
        begin += size
        row += count


def whiten(dec, table_ref, band_ref, alive):
    spectrum = jnp.dot(dec, table_ref[...], preferred_element_type=jnp.float32)
    real_part = spectrum[:, :HALF]
    imag_part = spectrum[:, HALF:]
    amplitude = jnp.sqrt(real_part * real_part + imag_part * imag_part)
    high = amplitude.astype(jnp.bfloat16)
    low = (amplitude - high.astype(jnp.float32)).astype(jnp.bfloat16)
    total = jnp.dot(
        jnp.concatenate([high, low], axis=1), band_ref[...], preferred_element_type=jnp.float32
    )
    factor = alive / (total * (1.0 / (2 * HW + 1)) + 1e-06)
    return jnp.concatenate([real_part * factor, imag_part * factor], axis=1).astype(jnp.bfloat16)


def late_kernel(
    sizes, orders, raw_ref, taps_ref, dead_ref, sources_ref, table_ref,
    out_ref, fir_ref, alive_ref, band_ref, select_ref,
):
    windows, rows, _ = out_ref.shape
    fill_fir(taps_ref, fir_ref)
    fill_alive(dead_ref, alive_ref)
    fill_band(band_ref)
    fill_selector(sizes, orders, sources_ref, select_ref)
    samples = jnp.concatenate(
        [raw_ref[:, w * SPAN - TAPS : (w + 1) * SPAN] for w in range(1, windows + 1)], axis=0
    )
    dec = nt_dot(samples, fir_ref[...]).astype(jnp.bfloat16)
    alive = jnp.concatenate([alive_ref[...]] * windows, axis=0)
    out_ref[...] = whiten(dec, table_ref, band_ref, alive).reshape(out_ref.shape)


def pick(select, white):
    return jnp.dot(select, white, preferred_element_type=jnp.float32).astype(jnp.bfloat16)


def first_kernel(
    raw_ref, hist_ref, fir_ref, table_ref, band_ref, alive_ref, late_ref, select_ref,
    panel_ref, white_ref,
):
    white_ref[1:] = late_ref[...]
    samples = jnp.concatenate([hist_ref[...], raw_ref[:, :SPAN]], axis=1)
    dec = nt_dot(samples, fir_ref[...]).astype(jnp.bfloat16)
    white_ref[0] = whiten(dec, table_ref, band_ref, alive_ref[...])
    select = select_ref[: panel_ref.shape[1]]
    for w in range(white_ref.shape[0]):
        panel_ref[w] = pick(select, white_ref[w])


def panels_kernel(skip, groups, select_ref, white_ref, *refs):
    own_refs, other_refs = refs[: len(groups)], refs[len(groups) :]
    for w in range(white_ref.shape[0]):
        chosen = pick(select_ref[skip:], white_ref[w])
        row = 0
        for group, own_ref, other_ref in zip(groups, own_refs, other_refs):
            place = 0
            for count in group:
                own_ref[w, place : place + count] = chosen[row : row + count]
                other_ref[w, place : place + count] = chosen[row + count : row + 2 * count]
                row += 2 * count
                place += count


def merge_kernel(*refs):
    groups = len(refs) // 3
    for own_ref, sib_ref, panel_ref in zip(refs[:groups], refs[groups : 2 * groups], refs[2 * groups :]):
        panel_ref[0] = own_ref[...]
        panel_ref[1] = sib_ref[...]


def gate_kernel(table_ref, out_ref):
    out_ref[...] = jnp.zeros_like(out_ref)


def split_kernel(panel_ref, recv_ref, keep_ref, send_ref):
    count = keep_ref.shape[1]
    keep_ref[...] = panel_ref[:, :count] + recv_ref[:, :count]
    send_ref[...] = panel_ref[:, count:] + recv_ref[:, count:]


def product_kernel(sources, begin, white_ref, white_sib_ref, cos_ref, sin_ref, out_ref):
    windows = white_ref.shape[0]
    count = out_ref.shape[0]
    cos_lag = cos_ref[...][None]
    sin_lag = sin_ref[...][None]
    white = jnp.concatenate(
        [ref[w] for ref in (white_ref, white_sib_ref) for w in range(windows)], axis=1
    )
    parts = []
    for side in range(2):
        for w in range(windows):
            source = sources(side, w, begin // NLAG, count // NLAG)
            real_src = source[:, None, :HALF]
            imag_src = source[:, None, HALF:]
            for part in (
                real_src * cos_lag + imag_src * sin_lag,
                imag_src * cos_lag - real_src * sin_lag,
            ):
                parts.append(part.reshape(count, HALF).astype(jnp.bfloat16))
    out_ref[...] = nt_dot(jnp.concatenate(parts, axis=1), white).astype(out_ref.dtype)


def taken_kernel(first, own_ref, sib_ref, *refs):
    def sources(side, w, begin, count):
        return (own_ref, sib_ref)[side][w, begin : begin + count].astype(jnp.float32)

    product_kernel(sources, first, *refs)


def summed_kernel(place, first, panel_ref, recv_ref, *refs):
    def sources(side, w, begin, count):
        rows = slice(place + begin, place + begin + count)
        return panel_ref[side, w, rows].astype(jnp.float32) + recv_ref[side, w, rows].astype(jnp.float32)

    product_kernel(sources, first, *refs)


def halves_kernel(pieces, *refs):
    *parts, kept_ref, send_ref = refs
    place = 0
    for keep_ref, recv_ref, counts in zip(parts[::2], parts[1::2], pieces):
        row = 0
        for count in counts:
            half = count // 2
            for out_ref, begin in ((kept_ref, row), (send_ref, row + half)):
                rows = slice(begin, begin + half)
                value = keep_ref[rows, :] + recv_ref[rows, :].astype(jnp.float32)
                out_ref[place : place + half, :] = value.astype(out_ref.dtype)
            row += count
            place += half


def total_kernel(keep_ref, recv_ref, out_ref):
    out_ref[...] = keep_ref[...] + recv_ref[...].astype(jnp.float32)


def last_kernel(pieces, *refs):
    *parts, out_ref, late_ref, sems = refs
    parts = iter(parts)
    copies, place = [], 0
    for summed, places in sorted(pieces, key=lambda piece: not piece[0]):
        keep_ref = next(parts)
        recv_ref = None if summed else next(parts)
        row = 0
        for begin, count in places:
            source = keep_ref.at[row : row + count]
            if not summed:
                rows = slice(row, row + count)
                late_ref[place : place + count] = keep_ref[rows, :] + recv_ref[rows, :].astype(jnp.float32)
                source = late_ref.at[place : place + count]
                place += count
            copy = pltpu.make_async_copy(source, out_ref.at[begin : begin + count], sems.at[len(copies)])
            copy.start()
            copies.append(copy)
            row += count
    for copy in copies:
        copy.wait()


class Chain:
    def __init__(self):
        self.last = None

    def __call__(self, name, kernel, args, outs, scratch=(), gates=(), waits=(), limit=VMEM_LIMIT, first=VMEM, result=VMEM):
        args, gates = list(args), list(gates)
        order = [*waits] if self.last is None else [*waits, self.last]
        taken, passed = len(args), len(args) + len(gates) + len(order)

        def body(*refs):
            written = refs[passed : passed + len(outs)]
            kernel(*refs[:taken], *written, *refs[passed + len(outs) + len(gates) :])

        results = pl.pallas_call(
            body,
            out_shape=[*outs, *(jax.ShapeDtypeStruct(g.shape, g.dtype) for g in gates)],
            in_specs=[first] + [VMEM] * (taken - 1) + [ANY] * (len(gates) + len(order)),
            out_specs=[result] * len(outs) + [ANY] * len(gates),
            input_output_aliases={taken + i: len(outs) + i for i in range(len(gates))},
            scratch_shapes=list(scratch),
            compiler_params=params(limit),
            cost_estimate=cost(1e9 * COSTS.get(name, BASE_COST), 1e4),
            name=name,
        )(*args, *gates, *order)
        self.last = results[0]
        return results


def local(raw_traces, fir_taps, sources, dead_flags):
    rows, samples = raw_traces.shape
    windows = samples // SPAN
    late = windows - 1
    time_parts = lax.axis_size("tm")
    chan_parts = lax.axis_size("chan")
    per_dest = VS // time_parts
    codes = time_parts // 2
    bits = [1 << i for i in range(1, time_parts.bit_length() - 1)]
    sizes, firsts, seconds, thirds, plan = CHUNKS, FIRST, SECOND, THIRD, PLAN
    across_groups = ACROSS
    if per_dest != sum(CHUNKS) or len(bits) != 3:
        sizes, firsts = (per_dest // 2,) * 2, (0, 0)
        seconds = thirds = ((0,), (1,))
        across_groups = ((1,),)
        plan = [("split", 0, (), ()), ("merge", 0, (1,), ())]
        plan += [(kind, q, (), ()) for q in (0, 1) for kind in ("send", "keep")]
        final = "third" + "+" * (len(bits) - 3)
        plan += [(name, q, (), ()) for name in ("second", *(final[:5 + i] for i in range(len(final) - 4))) for q in (0, 1)]
    final = "third" + "+" * (len(bits) - 3)
    orders = [[bits[first], *bits[:first], *bits[first + 1 :]] for first in firsts]
    counts = [size * codes for size in sizes]
    bf16, f32 = jnp.bfloat16, jnp.float32
    shape = jax.ShapeDtypeStruct
    chain = Chain()

    (tail,) = chain(
        "history", history_kernel, [pltpu.with_memory_space_constraint(raw_traces, pltpu.HBM)], [shape((rows, TAPS), bf16)], [pltpu.SemaphoreType.DMA],
        first=ANY,
    )
    history = lax.ppermute(tail, "tm", [(i, i + 1) for i in range(time_parts - 1)])

    table = jnp.asarray(dft_table())
    late_white, fir, alive, band, select = chain(
        "late",
        functools.partial(late_kernel, sizes, orders),
        [raw_traces, fir_taps.reshape(1, -1), dead_flags.reshape(1, -1), sources.reshape(1, -1), table],
        [
            shape((late, rows, TD), bf16),
            shape((TD, SPAN + TAPS), bf16),
            shape((rows, HALF), f32),
            shape((TD, HALF), bf16),
            shape((VS, rows), bf16),
        ],
    )
    panel, white = chain(
        "first",
        first_kernel,
        [raw_traces, history, fir, table, band, alive, late_white, select],
        [shape((windows, 2 * counts[0], TD), bf16), shape((windows, rows, TD), bf16)],
    )
    _, white = chain("gate", gate_kernel, [table], [shape((8, HALF), f32)], gates=[white])
    white_sib = swap(white, "tm", 1)
    members = [[counts[chunk] for chunk in group] for group in across_groups]
    rest = [shape((windows, sum(group), TD), bf16) for group in members]
    parts = chain("panels", functools.partial(panels_kernel, 2 * counts[0], members), [select, white], rest + rest)
    own, sib = parts[: len(rest)], [swap(other, "tm", 1) for other in parts[len(rest) :]]
    tables = [jnp.asarray(t) for t in lag_tables(1.0 / math.sqrt(time_parts * windows * TD))]
    spectra = [white, white_sib, *tables]

    def across(panel):
        if chan_parts == 2:
            return swap(panel, "chan", 1)
        return lax.psum(panel, "chan") - panel

    panels = {0: panel}
    arrived = {}
    state, pieces, moved = {}, {}, {}
    for kind, q, leaving, waits in plan:
        name = f"{kind}_{q}"
        gates = [panels[g] for g in leaving if g in panels]
        held = [moved[key] for key in waits if key in moved]
        call = functools.partial(chain, name, gates=gates, waits=held)
        if kind == "split":
            half = shape((windows, counts[0], TD), bf16)
            keep, send, *let = call(split_kernel, [panel, across(panel)], [half, half])
            taken = [keep, swap(send, "tm", 1)]
        elif kind == "merge":
            totals = [sum(counts[chunk] for chunk in group) for group in across_groups]
            made = call(merge_kernel, [*own, *sib], [shape((2, windows, total, TD), bf16) for total in totals])
            panels.update(enumerate(made, 1))
            let = []
        elif kind in ("send", "keep"):
            half = counts[q] * NLAG // 2
            args, kernel = taken, taken_kernel
            for g, group in enumerate(across_groups, 1):
                if q in group:
                    place = sum(counts[chunk] for chunk in group if chunk < q)
                    args, kernel = [panels[g], arrived[g]], functools.partial(summed_kernel, place)
            made, *let = call(
                functools.partial(kernel, half if kind == "send" else 0), [*args, *spectra],
                [shape((half, rows), bf16 if kind == "send" else f32)],
            )
            if kind == "send":
                moved["first", q] = swap(made, "tm", orders[q][0])
                pieces["first", q] = [half]
            else:
                state["first", q] = made, moved["first", q]
        elif kind == "sum":
            keep, recv = state["third", q]
            total, *let = call(total_kernel, [keep, recv], [shape(keep.shape, f32)])
            state["third", q] = total, None
        else:
            before, groups = {"second": ("first", seconds), "third": ("second", thirds)}.get(kind, (kind[:-1], thirds))
            members = [(before, member) for member in groups[q]]
            if before.startswith("third"):
                members = [(before, q)]
            split = [pieces[m] for m in members]
            half = sum(map(sum, split)) // 2
            keep, send, *let = call(
                functools.partial(halves_kernel, split), [x for m in members for x in state[m]],
                [shape((half, rows), f32), shape((half, rows), bf16)],
            )
            pieces[kind, q] = [count // 2 for part in split for count in part]
            chunk = groups[q][0] if kind == "second" else seconds[groups[q][0]][0]
            stage = 1 if kind == "second" else 2 + kind.count("+")
            moved[kind, q] = swap(send, "tm", orders[chunk][stage])
            state[kind, q] = keep, moved[kind, q]
        panels.update(zip(leaving, let))
        for g in leaving:
            moved["y", g] = arrived[g] = across(panels[g])

    starts = [sum(sizes[:q]) * NLAG for q in range(len(sizes))]
    args, places = [], []
    for q, group in sorted(enumerate(thirds), key=lambda item: state[final, item[0]][1] is not None):
        args += [x for x in state[final, q] if x is not None]
        chunks = [chunk for member in group for chunk in seconds[member]]
        places.append((state[final, q][1] is None, [(starts[chunk], sizes[chunk] * NLAG) for chunk in chunks]))
    (stacked,) = chain(
        "last",
        functools.partial(last_kernel, places),
        args,
        [shape((per_dest * NLAG, rows), f32)],
        [pltpu.VMEM((per_dest * NLAG, rows), f32), pltpu.SemaphoreType.DMA((len(sizes),))],
        result=ANY,
    )
    return stacked.reshape(per_dest, NLAG, rows)


def solution(mesh):
    return jax.shard_map(
        local,
        mesh=mesh,
        in_specs=(P("chan", "tm"), P(), P(), P("chan")),
        out_specs=P("tm", None, "chan"),
        check_vma=False,
    )
```

```python
import functools
import math

import jax
import jax.numpy as jnp
import numpy as np
from jax import lax
from jax.experimental import pallas as pl
from jax.experimental.pallas import tpu as pltpu
from jax.sharding import PartitionSpec as P

VS = 512
TD = 256
HALF = TD // 2
NLAG = 8
HW = 32
TAPS = 128
DECIM = 4
SPAN = DECIM * TD
VMEM_LIMIT = 20 * 1024 * 1024
CHUNKS = (6, 6, 6, 8, 6)
FIRST = (1, 1, 0, 1, 0)
SECOND = ((2,), (4,), (0, 1), (3,))
THIRD = ((2,), (0,), (3,), (1,))
ACROSS = ((1,), (2,), (3,), (4,))
PLAN = (
    ('merge', 0, (1, 2, 3), ()),
    ('split', 0, (), ()),
    ('send', 0, (), ()),
    ('keep', 0, (4,), ()),
    ('send', 1, (), ()),
    ('keep', 1, (), ()),
    ('send', 2, (), (('y', 2),)),
    ('keep', 2, (), (('first', 0),)),
    ('send', 3, (), (('y', 3),)),
    ('second', 2, (), ()),
    ('keep', 3, (), ()),
    ('send', 4, (), (('y', 4),)),
    ('second', 0, (), ()),
    ('third', 0, (), (('first', 2),)),
    ('second', 3, (), (('first', 3),)),
    ('keep', 4, (), ()),
    ('third', 1, (), (('second', 0),)),
    ('second', 1, (), (('first', 4), ('second', 2))),
    ('sum', 0, (), (('third', 0),)),
    ('third', 2, (), (('second', 3),)),
    ('sum', 1, (), (('third', 1),)),
    ('third', 3, (), (('second', 1),)),
    ('sum', 2, (), ()),
)
BASE_COST = 0.05
COSTS = {
    'merge_0': 0.52,
    'split_0': 15,
    'send_0': 0.5,
    'keep_0': 0.182,
    'send_2': 15,
    'keep_2': 0.347,
    'send_3': 0.277,
    'second_2': 0.191,
    'keep_3': 0.112,
    'send_4': 0.275,
    'second_0': 0.191,
    'keep_4': 0.11,
    'third_0': 0.286,
    'second_3': 0.191,
    'third_1': 0.286,
    'second_1': 2,
    'sum_0': 0.027,
    'third_2': 0.304,
    'sum_1': 1,
    'third_3': 0.373,
    'sum_2': 0.293,
    'panels': 0.05,
    'gate': 4,
    'first': 0.5,
    'send_1': 0.05,
    'keep_1': 0.05,
}

VMEM = pl.BlockSpec(memory_space=pltpu.VMEM)
ANY = pl.BlockSpec(memory_space=pl.ANY)


def params(limit=VMEM_LIMIT):
    return pltpu.CompilerParams(vmem_limit_bytes=limit)


def cost(flops, nbytes):
    return pl.CostEstimate(flops=int(flops), bytes_accessed=int(nbytes), transcendentals=0)


def swap(value, axis, bit):
    return lax.ppermute(value, axis, [(i, i ^ bit) for i in range(lax.axis_size(axis))])


def dft_table():
    phase = np.arange(TD)[:, None] * np.arange(HALF)[None, :] % TD
    angles = np.float32(2.0 * math.pi / TD) * phase.astype(np.float32)
    return np.concatenate([np.cos(angles), -np.sin(angles)], axis=1).astype(jnp.bfloat16)


def lag_tables(gain):
    phase = (np.arange(NLAG) - NLAG // 2)[:, None] * np.arange(HALF)[None, :] % TD
    angles = 2.0 * math.pi / TD * phase.astype(np.float64)
    return (gain * np.cos(angles)).astype(np.float32), (gain * np.sin(angles)).astype(np.float32)


def nt_dot(left, right):
    return lax.dot_general(left, right, (((1,), (1,)), ((), ())), preferred_element_type=jnp.float32)


def history_kernel(raw_ref, out_ref, sem):
    samples = raw_ref.shape[1]
    copy = pltpu.make_async_copy(raw_ref.at[:, samples - TAPS :], out_ref, sem)
    copy.start()
    copy.wait()


def fill_fir(taps_ref, fir_ref):
    rows = TAPS // DECIM
    taps = jnp.broadcast_to(taps_ref[...].astype(jnp.float32), (rows, TAPS))
    padded = jnp.concatenate([taps, jnp.zeros_like(taps)], axis=1)
    base = pltpu.roll(padded, 1, 1, stride=DECIM, stride_axis=0).astype(jnp.bfloat16)
    fir_ref[...] = jnp.zeros_like(fir_ref)
    for i in range(TD // rows):
        fir_ref[rows * i : rows * (i + 1), TAPS * i : TAPS * (i + 2)] = base


def fill_alive(dead_ref, alive_ref):
    alive = 1.0 - dead_ref[...].astype(jnp.float32)
    for i in range(0, alive_ref.shape[0], HALF):
        alive_ref[i : i + HALF, :] = jnp.broadcast_to(alive[:, i : i + HALF], (HALF, HALF)).T


def fill_band(band_ref):
    bins = lax.broadcasted_iota(jnp.int32, band_ref.shape, 0) & (HALF - 1)
    apart = jnp.abs(bins - lax.broadcasted_iota(jnp.int32, band_ref.shape, 1))
    band_ref[...] = jnp.where(apart <= HW, 1.0, 0.0).astype(jnp.bfloat16)


def fill_selector(sizes, orders, sources_ref, select_ref):
    rows = select_ref.shape[1]
    me = lax.axis_index("tm")
    first_chan = lax.axis_index("chan") * rows
    per_dest = sum(sizes)
    codes = 1 << len(orders[0])
    channels = sources_ref[...].astype(jnp.float32)
    begin, row = 0, 0
    for size, bits in zip(sizes, orders):
        count = 2 * codes * size
        index = lax.broadcasted_iota(jnp.int32, (count, VS), 0)
        scale = (1 << 16) // size + 1
        piece = lax.shift_right_logical(index * scale, 16)
        relative = lax.shift_right_logical(piece, len(bits))
        for place, bit in enumerate(bits):
            relative = relative + bit * (lax.shift_right_logical(piece, len(bits) - 1 - place) & 1)
        wanted = per_dest * jnp.bitwise_xor(relative, me) + begin + (index - size * piece)
        match = wanted == lax.broadcasted_iota(jnp.int32, (count, VS), 1)
        chosen = jnp.sum(jnp.where(match, channels, 0.0), axis=1, keepdims=True)
        place = chosen.astype(jnp.int32) - first_chan
        hit = place == lax.broadcasted_iota(jnp.int32, (count, rows), 1)
        select_ref[row : row + count, :] = jnp.where(hit, 1.0, 0.0).astype(jnp.bfloat16)
        begin += size
        row += count


def whiten(dec, table_ref, band_ref, alive):
    spectrum = jnp.dot(dec, table_ref[...], preferred_element_type=jnp.float32)
    real_part = spectrum[:, :HALF]
    imag_part = spectrum[:, HALF:]
    amplitude = jnp.sqrt(real_part * real_part + imag_part * imag_part)
    high = amplitude.astype(jnp.bfloat16)
    low = (amplitude - high.astype(jnp.float32)).astype(jnp.bfloat16)
    total = jnp.dot(
        jnp.concatenate([high, low], axis=1), band_ref[...], preferred_element_type=jnp.float32
    )
    factor = alive / (total * (1.0 / (2 * HW + 1)) + 1e-06)
    return jnp.concatenate([real_part * factor, imag_part * factor], axis=1).astype(jnp.bfloat16)


def late_kernel(
    sizes, orders, raw_ref, taps_ref, dead_ref, sources_ref, table_ref,
    out_ref, fir_ref, alive_ref, band_ref, select_ref,
):
    windows, rows, _ = out_ref.shape
    fill_fir(taps_ref, fir_ref)
    fill_alive(dead_ref, alive_ref)
    fill_band(band_ref)
    fill_selector(sizes, orders, sources_ref, select_ref)
    samples = jnp.concatenate(
        [raw_ref[:, w * SPAN - TAPS : (w + 1) * SPAN] for w in range(1, windows + 1)], axis=0
    )
    dec = nt_dot(samples, fir_ref[...]).astype(jnp.bfloat16)
    alive = jnp.concatenate([alive_ref[...]] * windows, axis=0)
    out_ref[...] = whiten(dec, table_ref, band_ref, alive).reshape(out_ref.shape)


def pick(select, white):
    return jnp.dot(select, white, preferred_element_type=jnp.float32).astype(jnp.bfloat16)


def first_kernel(
    raw_ref, hist_ref, fir_ref, table_ref, band_ref, alive_ref, late_ref, select_ref,
    panel_ref, white_ref,
):
    white_ref[1:] = late_ref[...]
    samples = jnp.concatenate([hist_ref[...], raw_ref[:, :SPAN]], axis=1)
    dec = nt_dot(samples, fir_ref[...]).astype(jnp.bfloat16)
    white_ref[0] = whiten(dec, table_ref, band_ref, alive_ref[...])
    select = select_ref[: panel_ref.shape[1]]
    for w in range(white_ref.shape[0]):
        panel_ref[w] = pick(select, white_ref[w])


def panels_kernel(skip, groups, select_ref, white_ref, *refs):
    own_refs, other_refs = refs[: len(groups)], refs[len(groups) :]
    for w in range(white_ref.shape[0]):
        chosen = pick(select_ref[skip:], white_ref[w])
        row = 0
        for group, own_ref, other_ref in zip(groups, own_refs, other_refs):
            place = 0
            for count in group:
                own_ref[w, place : place + count] = chosen[row : row + count]
                other_ref[w, place : place + count] = chosen[row + count : row + 2 * count]
                row += 2 * count
                place += count


def merge_kernel(*refs):
    groups = len(refs) // 3
    for own_ref, sib_ref, panel_ref in zip(refs[:groups], refs[groups : 2 * groups], refs[2 * groups :]):
        panel_ref[0] = own_ref[...]
        panel_ref[1] = sib_ref[...]


def gate_kernel(table_ref, out_ref):
    out_ref[...] = jnp.zeros_like(out_ref)


def split_kernel(panel_ref, recv_ref, keep_ref, send_ref):
    count = keep_ref.shape[1]
    keep_ref[...] = panel_ref[:, :count] + recv_ref[:, :count]
    send_ref[...] = panel_ref[:, count:] + recv_ref[:, count:]


def product_kernel(sources, begin, white_ref, white_sib_ref, cos_ref, sin_ref, out_ref):
    windows = white_ref.shape[0]
    count = out_ref.shape[0]
    cos_lag = cos_ref[...][None]
    sin_lag = sin_ref[...][None]
    white = jnp.concatenate(
        [ref[w] for ref in (white_ref, white_sib_ref) for w in range(windows)], axis=1
    )
    parts = []
    for side in range(2):
        for w in range(windows):
            source = sources(side, w, begin // NLAG, count // NLAG)
            real_src = source[:, None, :HALF]
            imag_src = source[:, None, HALF:]
            for part in (
                real_src * cos_lag + imag_src * sin_lag,
                imag_src * cos_lag - real_src * sin_lag,
            ):
                parts.append(part.reshape(count, HALF).astype(jnp.bfloat16))
    out_ref[...] = nt_dot(jnp.concatenate(parts, axis=1), white).astype(out_ref.dtype)


def taken_kernel(first, own_ref, sib_ref, *refs):
    def sources(side, w, begin, count):
        return (own_ref, sib_ref)[side][w, begin : begin + count].astype(jnp.float32)

    product_kernel(sources, first, *refs)


def summed_kernel(place, first, panel_ref, recv_ref, *refs):
    def sources(side, w, begin, count):
        rows = slice(place + begin, place + begin + count)
        return panel_ref[side, w, rows].astype(jnp.float32) + recv_ref[side, w, rows].astype(jnp.float32)

    product_kernel(sources, first, *refs)


def halves_kernel(pieces, *refs):
    *parts, kept_ref, send_ref = refs
    place = 0
    for keep_ref, recv_ref, counts in zip(parts[::2], parts[1::2], pieces):
        row = 0
        for count in counts:
            half = count // 2
            for out_ref, begin in ((kept_ref, row), (send_ref, row + half)):
                rows = slice(begin, begin + half)
                value = keep_ref[rows, :] + recv_ref[rows, :].astype(jnp.float32)
                out_ref[place : place + half, :] = value.astype(out_ref.dtype)
            row += count
            place += half


def total_kernel(keep_ref, recv_ref, out_ref):
    out_ref[...] = keep_ref[...] + recv_ref[...].astype(jnp.float32)


def last_kernel(pieces, *refs):
    *parts, out_ref, late_ref, sems = refs
    parts = iter(parts)
    copies, place = [], 0
    for summed, places in sorted(pieces, key=lambda piece: not piece[0]):
        keep_ref = next(parts)
        recv_ref = None if summed else next(parts)
        row = 0
        for begin, count in places:
            source = keep_ref.at[row : row + count]
            if not summed:
                rows = slice(row, row + count)
                late_ref[place : place + count] = keep_ref[rows, :] + recv_ref[rows, :].astype(jnp.float32)
                source = late_ref.at[place : place + count]
                place += count
            copy = pltpu.make_async_copy(source, out_ref.at[begin : begin + count], sems.at[len(copies)])
            copy.start()
            copies.append(copy)
            row += count
    for copy in copies:
        copy.wait()


class Chain:
    def __init__(self):
        self.last = None

    def __call__(self, name, kernel, args, outs, scratch=(), gates=(), waits=(), limit=VMEM_LIMIT, first=VMEM, result=VMEM):
        args, gates = list(args), list(gates)
        order = [*waits] if self.last is None else [*waits, self.last]
        taken, passed = len(args), len(args) + len(gates) + len(order)

        def body(*refs):
            written = refs[passed : passed + len(outs)]
            kernel(*refs[:taken], *written, *refs[passed + len(outs) + len(gates) :])

        results = pl.pallas_call(
            body,
            out_shape=[*outs, *(jax.ShapeDtypeStruct(g.shape, g.dtype) for g in gates)],
            in_specs=[first] + [VMEM] * (taken - 1) + [ANY] * (len(gates) + len(order)),
            out_specs=[result] * len(outs) + [ANY] * len(gates),
            input_output_aliases={taken + i: len(outs) + i for i in range(len(gates))},
            scratch_shapes=list(scratch),
            compiler_params=params(limit),
            cost_estimate=cost(1e9 * COSTS.get(name, BASE_COST), 1e4),
            name=name,
        )(*args, *gates, *order)
        self.last = results[0]
        return results


def local(raw_traces, fir_taps, sources, dead_flags):
    rows, samples = raw_traces.shape
    windows = samples // SPAN
    late = windows - 1
    time_parts = lax.axis_size("tm")
    chan_parts = lax.axis_size("chan")
    per_dest = VS // time_parts
    codes = time_parts // 2
    bits = [1 << i for i in range(1, time_parts.bit_length() - 1)]
    sizes, firsts, seconds, thirds, plan = CHUNKS, FIRST, SECOND, THIRD, PLAN
    across_groups = ACROSS
    if per_dest != sum(CHUNKS) or len(bits) != 3:
        sizes, firsts = (per_dest // 2,) * 2, (0, 0)
        seconds = thirds = ((0,), (1,))
        across_groups = ((1,),)
        plan = [("split", 0, (), ()), ("merge", 0, (1,), ())]
        plan += [(kind, q, (), ()) for q in (0, 1) for kind in ("send", "keep")]
        final = "third" + "+" * (len(bits) - 3)
        plan += [(name, q, (), ()) for name in ("second", *(final[:5 + i] for i in range(len(final) - 4))) for q in (0, 1)]
    final = "third" + "+" * (len(bits) - 3)
    orders = [[bits[first], *bits[:first], *bits[first + 1 :]] for first in firsts]
    counts = [size * codes for size in sizes]
    bf16, f32 = jnp.bfloat16, jnp.float32
    shape = jax.ShapeDtypeStruct
    chain = Chain()

    (tail,) = chain(
        "history", history_kernel, [pltpu.with_memory_space_constraint(raw_traces, pltpu.HBM)], [shape((rows, TAPS), bf16)], [pltpu.SemaphoreType.DMA],
        first=ANY,
    )
    history = lax.ppermute(tail, "tm", [(i, i + 1) for i in range(time_parts - 1)])

    table = jnp.asarray(dft_table())
    late_white, fir, alive, band, select = chain(
        "late",
        functools.partial(late_kernel, sizes, orders),
        [raw_traces, fir_taps.reshape(1, -1), dead_flags.reshape(1, -1), sources.reshape(1, -1), table],
        [
            shape((late, rows, TD), bf16),
            shape((TD, SPAN + TAPS), bf16),
            shape((rows, HALF), f32),
            shape((TD, HALF), bf16),
            shape((VS, rows), bf16),
        ],
    )
    panel, white = chain(
        "first",
        first_kernel,
        [raw_traces, history, fir, table, band, alive, late_white, select],
        [shape((windows, 2 * counts[0], TD), bf16), shape((windows, rows, TD), bf16)],
    )
    _, white = chain("gate", gate_kernel, [table], [shape((8, HALF), f32)], gates=[white])
    white_sib = swap(white, "tm", 1)
    members = [[counts[chunk] for chunk in group] for group in across_groups]
    rest = [shape((windows, sum(group), TD), bf16) for group in members]
    parts = chain("panels", functools.partial(panels_kernel, 2 * counts[0], members), [select, white], rest + rest)
    own, sib = parts[: len(rest)], [swap(other, "tm", 1) for other in parts[len(rest) :]]
    tables = [jnp.asarray(t) for t in lag_tables(1.0 / math.sqrt(time_parts * windows * TD))]
    spectra = [white, white_sib, *tables]

    def across(panel):
        if chan_parts == 2:
            return swap(panel, "chan", 1)
        return lax.psum(panel, "chan") - panel

    panels = {0: panel}
    arrived = {}
    state, pieces, moved = {}, {}, {}
    for kind, q, leaving, waits in plan:
        name = f"{kind}_{q}"
        gates = [panels[g] for g in leaving if g in panels]
        held = [moved[key] for key in waits if key in moved]
        call = functools.partial(chain, name, gates=gates, waits=held)
        if kind == "split":
            half = shape((windows, counts[0], TD), bf16)
            keep, send, *let = call(split_kernel, [panel, across(panel)], [half, half])
            taken = [keep, swap(send, "tm", 1)]
        elif kind == "merge":
            totals = [sum(counts[chunk] for chunk in group) for group in across_groups]
            made = call(merge_kernel, [*own, *sib], [shape((2, windows, total, TD), bf16) for total in totals])
            panels.update(enumerate(made, 1))
            let = []
        elif kind in ("send", "keep"):
            half = counts[q] * NLAG // 2
            args, kernel = taken, taken_kernel
            for g, group in enumerate(across_groups, 1):
                if q in group:
                    place = sum(counts[chunk] for chunk in group if chunk < q)
                    args, kernel = [panels[g], arrived[g]], functools.partial(summed_kernel, place)
            made, *let = call(
                functools.partial(kernel, half if kind == "send" else 0), [*args, *spectra],
                [shape((half, rows), bf16 if kind == "send" else f32)],
            )
            if kind == "send":
                moved["first", q] = swap(made, "tm", orders[q][0])
                pieces["first", q] = [half]
            else:
                state["first", q] = made, moved["first", q]
        elif kind == "sum":
            keep, recv = state["third", q]
            total, *let = call(total_kernel, [keep, recv], [shape(keep.shape, f32)])
            state["third", q] = total, None
        else:
            before, groups = {"second": ("first", seconds), "third": ("second", thirds)}.get(kind, (kind[:-1], thirds))
            members = [(before, member) for member in groups[q]]
            if before.startswith("third"):
                members = [(before, q)]
            split = [pieces[m] for m in members]
            half = sum(map(sum, split)) // 2
            keep, send, *let = call(
                functools.partial(halves_kernel, split), [x for m in members for x in state[m]],
                [shape((half, rows), f32), shape((half, rows), bf16)],
            )
            pieces[kind, q] = [count // 2 for part in split for count in part]
            chunk = groups[q][0] if kind == "second" else seconds[groups[q][0]][0]
            stage = 1 if kind == "second" else 2 + kind.count("+")
            moved[kind, q] = swap(send, "tm", orders[chunk][stage])
            state[kind, q] = keep, moved[kind, q]
        panels.update(zip(leaving, let))
        for g in leaving:
            moved["y", g] = arrived[g] = across(panels[g])

    starts = [sum(sizes[:q]) * NLAG for q in range(len(sizes))]
    args, places = [], []
    for q, group in sorted(enumerate(thirds), key=lambda item: state[final, item[0]][1] is not None):
        args += [x for x in state[final, q] if x is not None]
        chunks = [chunk for member in group for chunk in seconds[member]]
        places.append((state[final, q][1] is None, [(starts[chunk], sizes[chunk] * NLAG) for chunk in chunks]))
    (stacked,) = chain(
        "last",
        functools.partial(last_kernel, places),
        args,
        [shape((per_dest * NLAG, rows), f32)],
        [pltpu.VMEM((per_dest * NLAG, rows), f32), pltpu.SemaphoreType.DMA((len(sizes),))],
        result=ANY,
    )
    return stacked.reshape(per_dest, NLAG, rows)


def solution(mesh):
    return jax.shard_map(
        local,
        mesh=mesh,
        in_specs=(P("chan", "tm"), P(), P(), P("chan")),
        out_specs=P("tm", None, "chan"),
        check_vma=False,
    )
```

```python
import functools
import math

import jax
import jax.numpy as jnp
import numpy as np
from jax import lax
from jax.experimental import pallas as pl
from jax.experimental.pallas import tpu as pltpu
from jax.sharding import PartitionSpec as P

VS = 512
TD = 256
HALF = TD // 2
NLAG = 8
HW = 32
TAPS = 128
DECIM = 4
SPAN = DECIM * TD
VMEM_LIMIT = 20 * 1024 * 1024
CHUNKS = (6, 6, 6, 8, 6)
FIRST = (1, 1, 0, 1, 0)
SECOND = ((2,), (4,), (0, 1), (3,))
THIRD = ((2,), (0,), (3,), (1,))
ACROSS = ((1,), (2,), (3,), (4,))
PLAN = (
    ('merge', 0, (1, 2, 3), ()),
    ('split', 0, (), ()),
    ('send', 0, (), ()),
    ('keep', 0, (4,), ()),
    ('send', 1, (), ()),
    ('keep', 1, (), ()),
    ('send', 2, (), (('y', 2),)),
    ('keep', 2, (), (('first', 0),)),
    ('send', 3, (), (('y', 3),)),
    ('second', 2, (), ()),
    ('keep', 3, (), ()),
    ('send', 4, (), (('y', 4),)),
    ('second', 0, (), ()),
    ('third', 0, (), (('first', 2),)),
    ('second', 3, (), (('first', 3),)),
    ('keep', 4, (), ()),
    ('third', 1, (), (('second', 0),)),
    ('second', 1, (), (('first', 4), ('second', 2))),
    ('sum', 0, (), (('third', 0),)),
    ('third', 2, (), (('second', 3),)),
    ('sum', 1, (), (('third', 1),)),
    ('third', 3, (), (('second', 1),)),
    ('sum', 2, (), ()),
)
BASE_COST = 0.05
COSTS = {
    'merge_0': 0.52,
    'split_0': 15,
    'send_0': 0.5,
    'keep_0': 0.182,
    'send_2': 15,
    'keep_2': 0.347,
    'send_3': 0.277,
    'second_2': 0.191,
    'keep_3': 0.112,
    'send_4': 0.275,
    'second_0': 0.191,
    'keep_4': 0.11,
    'third_0': 0.286,
    'second_3': 0.191,
    'third_1': 0.286,
    'second_1': 2,
    'sum_0': 0.027,
    'third_2': 0.304,
    'sum_1': 1,
    'third_3': 0.373,
    'sum_2': 0.293,
    'panels': 0.05,
    'gate': 4,
    'first': 0.5,
    'send_1': 0.05,
    'keep_1': 0.05,
}

VMEM = pl.BlockSpec(memory_space=pltpu.VMEM)
ANY = pl.BlockSpec(memory_space=pl.ANY)


def params(limit=VMEM_LIMIT):
    return pltpu.CompilerParams(vmem_limit_bytes=limit)


def cost(flops, nbytes):
    return pl.CostEstimate(flops=int(flops), bytes_accessed=int(nbytes), transcendentals=0)


def swap(value, axis, bit):
    return lax.ppermute(value, axis, [(i, i ^ bit) for i in range(lax.axis_size(axis))])


def dft_table():
    phase = np.arange(TD)[:, None] * np.arange(HALF)[None, :] % TD
    angles = np.float32(2.0 * math.pi / TD) * phase.astype(np.float32)
    return np.concatenate([np.cos(angles), -np.sin(angles)], axis=1).astype(jnp.bfloat16)


def lag_tables(gain):
    phase = (np.arange(NLAG) - NLAG // 2)[:, None] * np.arange(HALF)[None, :] % TD
    angles = 2.0 * math.pi / TD * phase.astype(np.float64)
    return (gain * np.cos(angles)).astype(np.float32), (gain * np.sin(angles)).astype(np.float32)


def nt_dot(left, right):
    return lax.dot_general(left, right, (((1,), (1,)), ((), ())), preferred_element_type=jnp.float32)


def history_kernel(raw_ref, out_ref, sem):
    samples = raw_ref.shape[1]
    copy = pltpu.make_async_copy(raw_ref.at[:, samples - TAPS :], out_ref, sem)
    copy.start()
    copy.wait()


def fill_fir(taps_ref, fir_ref):
    rows = TAPS // DECIM
    taps = jnp.broadcast_to(taps_ref[...].astype(jnp.float32), (rows, TAPS))
    padded = jnp.concatenate([taps, jnp.zeros_like(taps)], axis=1)
    base = pltpu.roll(padded, 1, 1, stride=DECIM, stride_axis=0).astype(jnp.bfloat16)
    fir_ref[...] = jnp.zeros_like(fir_ref)
    for i in range(TD // rows):
        fir_ref[rows * i : rows * (i + 1), TAPS * i : TAPS * (i + 2)] = base


def fill_alive(dead_ref, alive_ref):
    alive = 1.0 - dead_ref[...].astype(jnp.float32)
    for i in range(0, alive_ref.shape[0], HALF):
        alive_ref[i : i + HALF, :] = jnp.broadcast_to(alive[:, i : i + HALF], (HALF, HALF)).T


def fill_band(band_ref):
    bins = lax.broadcasted_iota(jnp.int32, band_ref.shape, 0) & (HALF - 1)
    apart = jnp.abs(bins - lax.broadcasted_iota(jnp.int32, band_ref.shape, 1))
    band_ref[...] = jnp.where(apart <= HW, 1.0, 0.0).astype(jnp.bfloat16)


def fill_selector(sizes, orders, chunks, sources_ref, select_ref):
    rows = select_ref.shape[1]
    me = lax.axis_index("tm")
    first_chan = lax.axis_index("chan") * rows
    per_dest = sum(sizes)
    codes = 1 << len(orders[0])
    channels = sources_ref[...].astype(jnp.float32)
    begin, row = 0, 0
    for chunk, (size, bits) in enumerate(zip(sizes, orders)):
        if chunk not in chunks:
            begin += size
            continue
        count = 2 * codes * size
        index = lax.broadcasted_iota(jnp.int32, (count, VS), 0)
        scale = (1 << 16) // size + 1
        piece = lax.shift_right_logical(index * scale, 16)
        relative = lax.shift_right_logical(piece, len(bits))
        for place, bit in enumerate(bits):
            relative = relative + bit * (lax.shift_right_logical(piece, len(bits) - 1 - place) & 1)
        wanted = per_dest * jnp.bitwise_xor(relative, me) + begin + (index - size * piece)
        match = wanted == lax.broadcasted_iota(jnp.int32, (count, VS), 1)
        chosen = jnp.sum(jnp.where(match, channels, 0.0), axis=1, keepdims=True)
        place = chosen.astype(jnp.int32) - first_chan
        hit = place == lax.broadcasted_iota(jnp.int32, (count, rows), 1)
        select_ref[row : row + count, :] = jnp.where(hit, 1.0, 0.0).astype(jnp.bfloat16)
        begin += size
        row += count


def whiten(dec, table_ref, band_ref, alive):
    spectrum = jnp.dot(dec, table_ref[...], preferred_element_type=jnp.float32)
    real_part = spectrum[:, :HALF]
    imag_part = spectrum[:, HALF:]
    amplitude = jnp.sqrt(real_part * real_part + imag_part * imag_part)
    high = amplitude.astype(jnp.bfloat16)
    low = (amplitude - high.astype(jnp.float32)).astype(jnp.bfloat16)
    total = jnp.dot(
        jnp.concatenate([high, low], axis=1), band_ref[...], preferred_element_type=jnp.float32
    )
    factor = alive / (total * (1.0 / (2 * HW + 1)) + 1e-06)
    return jnp.concatenate([real_part * factor, imag_part * factor], axis=1).astype(jnp.bfloat16)


def late_kernel(
    sizes, orders, raw_ref, taps_ref, dead_ref, sources_ref, table_ref,
    out_ref, fir_ref, alive_ref, band_ref, select_ref,
):
    windows, rows, _ = out_ref.shape
    fill_fir(taps_ref, fir_ref)
    fill_alive(dead_ref, alive_ref)
    fill_band(band_ref)
    fill_selector(sizes, orders, (0,), sources_ref, select_ref)
    samples = jnp.concatenate(
        [raw_ref[:, w * SPAN - TAPS : (w + 1) * SPAN] for w in range(1, windows + 1)], axis=0
    )
    dec = nt_dot(samples, fir_ref[...]).astype(jnp.bfloat16)
    alive = jnp.concatenate([alive_ref[...]] * windows, axis=0)
    out_ref[...] = whiten(dec, table_ref, band_ref, alive).reshape(out_ref.shape)


def pick(select, white):
    return jnp.dot(select, white, preferred_element_type=jnp.float32).astype(jnp.bfloat16)


def first_kernel(
    raw_ref, hist_ref, fir_ref, table_ref, band_ref, alive_ref, late_ref, select_ref,
    panel_ref, white_ref,
):
    white_ref[1:] = late_ref[...]
    samples = jnp.concatenate([hist_ref[...], raw_ref[:, :SPAN]], axis=1)
    dec = nt_dot(samples, fir_ref[...]).astype(jnp.bfloat16)
    white_ref[0] = whiten(dec, table_ref, band_ref, alive_ref[...])
    select = select_ref[...]
    for w in range(white_ref.shape[0]):
        panel_ref[w] = pick(select, white_ref[w])


def panels_kernel(sizes, orders, groups, sources_ref, white_ref, *refs):
    *refs, select_ref = refs
    fill_selector(sizes, orders, range(1, len(sizes)), sources_ref, select_ref)
    own_refs, other_refs = refs[: len(groups)], refs[len(groups) :]
    for w in range(white_ref.shape[0]):
        chosen = pick(select_ref[...], white_ref[w])
        row = 0
        for group, own_ref, other_ref in zip(groups, own_refs, other_refs):
            place = 0
            for count in group:
                own_ref[w, place : place + count] = chosen[row : row + count]
                other_ref[w, place : place + count] = chosen[row + count : row + 2 * count]
                row += 2 * count
                place += count


def merge_kernel(*refs):
    groups = len(refs) // 3
    for own_ref, sib_ref, panel_ref in zip(refs[:groups], refs[groups : 2 * groups], refs[2 * groups :]):
        panel_ref[0] = own_ref[...]
        panel_ref[1] = sib_ref[...]


def gate_kernel(table_ref, out_ref):
    out_ref[...] = jnp.zeros_like(out_ref)


def split_kernel(panel_ref, recv_ref, keep_ref, send_ref):
    count = keep_ref.shape[1]
    keep_ref[...] = panel_ref[:, :count] + recv_ref[:, :count]
    send_ref[...] = panel_ref[:, count:] + recv_ref[:, count:]


def product_kernel(sources, begin, white_ref, white_sib_ref, cos_ref, sin_ref, out_ref):
    windows = white_ref.shape[0]
    count = out_ref.shape[0]
    cos_lag = cos_ref[...][None]
    sin_lag = sin_ref[...][None]
    white = jnp.concatenate(
        [ref[w] for ref in (white_ref, white_sib_ref) for w in range(windows)], axis=1
    )
    parts = []
    for side in range(2):
        for w in range(windows):
            source = sources(side, w, begin // NLAG, count // NLAG)
            real_src = source[:, None, :HALF]
            imag_src = source[:, None, HALF:]
            for part in (
                real_src * cos_lag + imag_src * sin_lag,
                imag_src * cos_lag - real_src * sin_lag,
            ):
                parts.append(part.reshape(count, HALF).astype(jnp.bfloat16))
    out_ref[...] = nt_dot(jnp.concatenate(parts, axis=1), white).astype(out_ref.dtype)


def taken_kernel(first, own_ref, sib_ref, *refs):
    def sources(side, w, begin, count):
        return (own_ref, sib_ref)[side][w, begin : begin + count].astype(jnp.float32)

    product_kernel(sources, first, *refs)


def summed_kernel(place, first, panel_ref, recv_ref, *refs):
    def sources(side, w, begin, count):
        rows = slice(place + begin, place + begin + count)
        return panel_ref[side, w, rows].astype(jnp.float32) + recv_ref[side, w, rows].astype(jnp.float32)

    product_kernel(sources, first, *refs)


def halves_kernel(pieces, *refs):
    *parts, kept_ref, send_ref = refs
    place = 0
    for keep_ref, recv_ref, counts in zip(parts[::2], parts[1::2], pieces):
        row = 0
        for count in counts:
            half = count // 2
            for out_ref, begin in ((kept_ref, row), (send_ref, row + half)):
                rows = slice(begin, begin + half)
                value = keep_ref[rows, :] + recv_ref[rows, :].astype(jnp.float32)
                out_ref[place : place + half, :] = value.astype(out_ref.dtype)
            row += count
            place += half


def total_kernel(keep_ref, recv_ref, out_ref):
    out_ref[...] = keep_ref[...] + recv_ref[...].astype(jnp.float32)


def last_kernel(pieces, *refs):
    *parts, out_ref, late_ref, sems = refs
    parts = iter(parts)
    copies, place = [], 0
    for summed, places in sorted(pieces, key=lambda piece: not piece[0]):
        keep_ref = next(parts)
        recv_ref = None if summed else next(parts)
        row = 0
        for begin, count in places:
            source = keep_ref.at[row : row + count]
            if not summed:
                rows = slice(row, row + count)
                late_ref[place : place + count] = keep_ref[rows, :] + recv_ref[rows, :].astype(jnp.float32)
                source = late_ref.at[place : place + count]
                place += count
            copy = pltpu.make_async_copy(source, out_ref.at[begin : begin + count], sems.at[len(copies)])
            copy.start()
            copies.append(copy)
            row += count
    for copy in copies:
        copy.wait()


class Chain:
    def __init__(self):
        self.last = None

    def __call__(self, name, kernel, args, outs, scratch=(), gates=(), waits=(), limit=VMEM_LIMIT, first=VMEM, result=VMEM):
        args, gates = list(args), list(gates)
        order = [*waits] if self.last is None else [*waits, self.last]
        taken, passed = len(args), len(args) + len(gates) + len(order)

        def body(*refs):
            written = refs[passed : passed + len(outs)]
            kernel(*refs[:taken], *written, *refs[passed + len(outs) + len(gates) :])

        results = pl.pallas_call(
            body,
            out_shape=[*outs, *(jax.ShapeDtypeStruct(g.shape, g.dtype) for g in gates)],
            in_specs=[first] + [VMEM] * (taken - 1) + [ANY] * (len(gates) + len(order)),
            out_specs=[result] * len(outs) + [ANY] * len(gates),
            input_output_aliases={taken + i: len(outs) + i for i in range(len(gates))},
            scratch_shapes=list(scratch),
            compiler_params=params(limit),
            cost_estimate=cost(1e9 * COSTS.get(name, BASE_COST), 1e4),
            name=name,
        )(*args, *gates, *order)
        self.last = results[0]
        return results


def local(raw_traces, fir_taps, sources, dead_flags):
    rows, samples = raw_traces.shape
    windows = samples // SPAN
    late = windows - 1
    time_parts = lax.axis_size("tm")
    chan_parts = lax.axis_size("chan")
    per_dest = VS // time_parts
    codes = time_parts // 2
    bits = [1 << i for i in range(1, time_parts.bit_length() - 1)]
    sizes, firsts, seconds, thirds, plan = CHUNKS, FIRST, SECOND, THIRD, PLAN
    across_groups = ACROSS
    if per_dest != sum(CHUNKS) or len(bits) != 3:
        sizes, firsts = (per_dest // 2,) * 2, (0, 0)
        seconds = thirds = ((0,), (1,))
        across_groups = ((1,),)
        plan = [("split", 0, (), ()), ("merge", 0, (1,), ())]
        plan += [(kind, q, (), ()) for q in (0, 1) for kind in ("send", "keep")]
        final = "third" + "+" * (len(bits) - 3)
        plan += [(name, q, (), ()) for name in ("second", *(final[:5 + i] for i in range(len(final) - 4))) for q in (0, 1)]
    final = "third" + "+" * (len(bits) - 3)
    orders = [[bits[first], *bits[:first], *bits[first + 1 :]] for first in firsts]
    counts = [size * codes for size in sizes]
    bf16, f32 = jnp.bfloat16, jnp.float32
    shape = jax.ShapeDtypeStruct
    chain = Chain()

    (tail,) = chain(
        "history", history_kernel, [pltpu.with_memory_space_constraint(raw_traces, pltpu.HBM)], [shape((rows, TAPS), bf16)], [pltpu.SemaphoreType.DMA],
        first=ANY,
    )
    history = lax.ppermute(tail, "tm", [(i, i + 1) for i in range(time_parts - 1)])

    table = jnp.asarray(dft_table())
    late_white, fir, alive, band, select = chain(
        "late",
        functools.partial(late_kernel, sizes, orders),
        [raw_traces, fir_taps.reshape(1, -1), dead_flags.reshape(1, -1), sources.reshape(1, -1), table],
        [
            shape((late, rows, TD), bf16),
            shape((TD, SPAN + TAPS), bf16),
            shape((rows, HALF), f32),
            shape((TD, HALF), bf16),
            shape((2 * counts[0], rows), bf16),
        ],
    )
    panel, white = chain(
        "first",
        first_kernel,
        [raw_traces, history, fir, table, band, alive, late_white, select],
        [shape((windows, 2 * counts[0], TD), bf16), shape((windows, rows, TD), bf16)],
    )
    _, white = chain("gate", gate_kernel, [table], [shape((8, HALF), f32)], gates=[white])
    white_sib = swap(white, "tm", 1)
    members = [[counts[chunk] for chunk in group] for group in across_groups]
    rest = [shape((windows, sum(group), TD), bf16) for group in members]
    parts = chain(
        "panels",
        functools.partial(panels_kernel, sizes, orders, members),
        [sources.reshape(1, -1), white],
        rest + rest,
        [pltpu.VMEM((VS - 2 * counts[0], rows), bf16)],
    )
    own, sib = parts[: len(rest)], [swap(other, "tm", 1) for other in parts[len(rest) :]]
    tables = [jnp.asarray(t) for t in lag_tables(1.0 / math.sqrt(time_parts * windows * TD))]
    spectra = [white, white_sib, *tables]

    def across(panel):
        if chan_parts == 2:
            return swap(panel, "chan", 1)
        return lax.psum(panel, "chan") - panel

    panels = {0: panel}
    arrived = {}
    state, pieces, moved = {}, {}, {}
    for kind, q, leaving, waits in plan:
        name = f"{kind}_{q}"
        gates = [panels[g] for g in leaving if g in panels]
        held = [moved[key] for key in waits if key in moved]
        call = functools.partial(chain, name, gates=gates, waits=held)
        if kind == "split":
            half = shape((windows, counts[0], TD), bf16)
            keep, send, *let = call(split_kernel, [panel, across(panel)], [half, half])
            taken = [keep, swap(send, "tm", 1)]
        elif kind == "merge":
            totals = [sum(counts[chunk] for chunk in group) for group in across_groups]
            made = call(merge_kernel, [*own, *sib], [shape((2, windows, total, TD), bf16) for total in totals])
            panels.update(enumerate(made, 1))
            let = []
        elif kind in ("send", "keep"):
            half = counts[q] * NLAG // 2
            args, kernel = taken, taken_kernel
            for g, group in enumerate(across_groups, 1):
                if q in group:
                    place = sum(counts[chunk] for chunk in group if chunk < q)
                    args, kernel = [panels[g], arrived[g]], functools.partial(summed_kernel, place)
            made, *let = call(
                functools.partial(kernel, half if kind == "send" else 0), [*args, *spectra],
                [shape((half, rows), bf16 if kind == "send" else f32)],
            )
            if kind == "send":
                moved["first", q] = swap(made, "tm", orders[q][0])
                pieces["first", q] = [half]
            else:
                state["first", q] = made, moved["first", q]
        elif kind == "sum":
            keep, recv = state["third", q]
            total, *let = call(total_kernel, [keep, recv], [shape(keep.shape, f32)])
            state["third", q] = total, None
        else:
            before, groups = {"second": ("first", seconds), "third": ("second", thirds)}.get(kind, (kind[:-1], thirds))
            members = [(before, member) for member in groups[q]]
            if before.startswith("third"):
                members = [(before, q)]
            split = [pieces[m] for m in members]
            half = sum(map(sum, split)) // 2
            keep, send, *let = call(
                functools.partial(halves_kernel, split), [x for m in members for x in state[m]],
                [shape((half, rows), f32), shape((half, rows), bf16)],
            )
            pieces[kind, q] = [count // 2 for part in split for count in part]
            chunk = groups[q][0] if kind == "second" else seconds[groups[q][0]][0]
            stage = 1 if kind == "second" else 2 + kind.count("+")
            moved[kind, q] = swap(send, "tm", orders[chunk][stage])
            state[kind, q] = keep, moved[kind, q]
        panels.update(zip(leaving, let))
        for g in leaving:
            moved["y", g] = arrived[g] = across(panels[g])

    starts = [sum(sizes[:q]) * NLAG for q in range(len(sizes))]
    args, places = [], []
    for q, group in sorted(enumerate(thirds), key=lambda item: state[final, item[0]][1] is not None):
        args += [x for x in state[final, q] if x is not None]
        chunks = [chunk for member in group for chunk in seconds[member]]
        places.append((state[final, q][1] is None, [(starts[chunk], sizes[chunk] * NLAG) for chunk in chunks]))
    (stacked,) = chain(
        "last",
        functools.partial(last_kernel, places),
        args,
        [shape((per_dest * NLAG, rows), f32)],
        [pltpu.VMEM((per_dest * NLAG, rows), f32), pltpu.SemaphoreType.DMA((len(sizes),))],
        result=ANY,
    )
    return stacked.reshape(per_dest, NLAG, rows)


def solution(mesh):
    return jax.shard_map(
        local,
        mesh=mesh,
        in_specs=(P("chan", "tm"), P(), P(), P("chan")),
        out_specs=P("tm", None, "chan"),
        check_vma=False,
    )
```

```python
import functools
import math

import jax
import jax.numpy as jnp
import numpy as np
from jax import lax
from jax.experimental import pallas as pl
from jax.experimental.pallas import tpu as pltpu
from jax.sharding import PartitionSpec as P

VS = 512
TD = 256
HALF = TD // 2
NLAG = 8
HW = 32
TAPS = 128
DECIM = 4
SPAN = DECIM * TD
VMEM_LIMIT = 20 * 1024 * 1024
CHUNKS = (6, 6, 6, 8, 6)
FIRST = (1, 1, 0, 1, 0)
SECOND = ((2,), (4,), (0, 1), (3,))
THIRD = ((2, 0), (3,), (1,))
ACROSS = ((1,), (2,), (3,), (4,))
PLAN = (
    ('merge', 0, (1, 2, 3), ()),
    ('split', 0, (), ()),
    ('send', 0, (), ()),
    ('keep', 0, (4,), ()),
    ('send', 1, (), ()),
    ('keep', 1, (), ()),
    ('send', 2, (), (('y', 2),)),
    ('keep', 2, (), ()),
    ('send', 3, (), (('y', 3), ('first', 0))),
    ('second', 2, (), ()),
    ('keep', 3, (), ()),
    ('send', 4, (), (('y', 4),)),
    ('second', 0, (), ()),
    ('second', 3, (), (('first', 3),)),
    ('keep', 4, (), ()),
    ('third', 0, (), ()),
    ('second', 1, (), (('first', 4), ('second', 2))),
    ('third', 1, (), ()),
    ('third', 2, (), ()),
    ('sum', 0, (), ()),
    ('sum', 1, (), ()),
)
BASE_COST = 0.05
COSTS = {
    'merge_0': 0.52,
    'split_0': 15,
    'send_0': 0.5,
    'keep_0': 0.182,
    'send_2': 15,
    'keep_2': 0.347,
    'send_3': 0.277,
    'second_2': 0.191,
    'keep_3': 0.112,
    'send_4': 0.275,
    'second_0': 0.191,
    'keep_4': 0.11,
    'second_3': 0.191,
    'second_1': 2,
    'panels': 0.05,
    'gate': 4,
    'first': 0.5,
    'send_1': 0.05,
    'keep_1': 0.05,
    'third_0': 0.05,
    'sum_0': 0.05,
    'third_1': 0.05,
    'sum_1': 0.05,
    'third_2': 0.05,
    'sum_2': 0.05,
}

VMEM = pl.BlockSpec(memory_space=pltpu.VMEM)
ANY = pl.BlockSpec(memory_space=pl.ANY)


def params(limit=VMEM_LIMIT):
    return pltpu.CompilerParams(vmem_limit_bytes=limit)


def cost(flops, nbytes):
    return pl.CostEstimate(flops=int(flops), bytes_accessed=int(nbytes), transcendentals=0)


def swap(value, axis, bit):
    return lax.ppermute(value, axis, [(i, i ^ bit) for i in range(lax.axis_size(axis))])


def dft_table():
    phase = np.arange(TD)[:, None] * np.arange(HALF)[None, :] % TD
    angles = np.float32(2.0 * math.pi / TD) * phase.astype(np.float32)
    return np.concatenate([np.cos(angles), -np.sin(angles)], axis=1).astype(jnp.bfloat16)


def lag_tables(gain):
    phase = (np.arange(NLAG) - NLAG // 2)[:, None] * np.arange(HALF)[None, :] % TD
    angles = 2.0 * math.pi / TD * phase.astype(np.float64)
    return (gain * np.cos(angles)).astype(np.float32), (gain * np.sin(angles)).astype(np.float32)


def nt_dot(left, right):
    return lax.dot_general(left, right, (((1,), (1,)), ((), ())), preferred_element_type=jnp.float32)


def history_kernel(raw_ref, out_ref, sem):
    samples = raw_ref.shape[1]
    copy = pltpu.make_async_copy(raw_ref.at[:, samples - TAPS :], out_ref, sem)
    copy.start()
    copy.wait()


def fill_fir(taps_ref, fir_ref):
    rows = TAPS // DECIM
    taps = jnp.broadcast_to(taps_ref[...].astype(jnp.float32), (rows, TAPS))
    padded = jnp.concatenate([taps, jnp.zeros_like(taps)], axis=1)
    base = pltpu.roll(padded, 1, 1, stride=DECIM, stride_axis=0).astype(jnp.bfloat16)
    fir_ref[...] = jnp.zeros_like(fir_ref)
    for i in range(TD // rows):
        fir_ref[rows * i : rows * (i + 1), TAPS * i : TAPS * (i + 2)] = base


def fill_alive(dead_ref, alive_ref):
    alive = 1.0 - dead_ref[...].astype(jnp.float32)
    for i in range(0, alive_ref.shape[0], HALF):
        alive_ref[i : i + HALF, :] = jnp.broadcast_to(alive[:, i : i + HALF], (HALF, HALF)).T


def fill_band(band_ref):
    bins = lax.broadcasted_iota(jnp.int32, band_ref.shape, 0) & (HALF - 1)
    apart = jnp.abs(bins - lax.broadcasted_iota(jnp.int32, band_ref.shape, 1))
    band_ref[...] = jnp.where(apart <= HW, 1.0, 0.0).astype(jnp.bfloat16)


def fill_selector(sizes, orders, sources_ref, select_ref):
    rows = select_ref.shape[1]
    me = lax.axis_index("tm")
    first_chan = lax.axis_index("chan") * rows
    per_dest = sum(sizes)
    codes = 1 << len(orders[0])
    channels = sources_ref[...].astype(jnp.float32)
    begin, row = 0, 0
    for size, bits in zip(sizes, orders):
        count = 2 * codes * size
        index = lax.broadcasted_iota(jnp.int32, (count, VS), 0)
        scale = (1 << 16) // size + 1
        piece = lax.shift_right_logical(index * scale, 16)
        relative = lax.shift_right_logical(piece, len(bits))
        for place, bit in enumerate(bits):
            relative = relative + bit * (lax.shift_right_logical(piece, len(bits) - 1 - place) & 1)
        wanted = per_dest * jnp.bitwise_xor(relative, me) + begin + (index - size * piece)
        match = wanted == lax.broadcasted_iota(jnp.int32, (count, VS), 1)
        chosen = jnp.sum(jnp.where(match, channels, 0.0), axis=1, keepdims=True)
        place = chosen.astype(jnp.int32) - first_chan
        hit = place == lax.broadcasted_iota(jnp.int32, (count, rows), 1)
        select_ref[row : row + count, :] = jnp.where(hit, 1.0, 0.0).astype(jnp.bfloat16)
        begin += size
        row += count


def whiten(dec, table_ref, band_ref, alive):
    spectrum = jnp.dot(dec, table_ref[...], preferred_element_type=jnp.float32)
    real_part = spectrum[:, :HALF]
    imag_part = spectrum[:, HALF:]
    amplitude = jnp.sqrt(real_part * real_part + imag_part * imag_part)
    high = amplitude.astype(jnp.bfloat16)
    low = (amplitude - high.astype(jnp.float32)).astype(jnp.bfloat16)
    total = jnp.dot(
        jnp.concatenate([high, low], axis=1), band_ref[...], preferred_element_type=jnp.float32
    )
    factor = alive / (total * (1.0 / (2 * HW + 1)) + 1e-06)
    return jnp.concatenate([real_part * factor, imag_part * factor], axis=1).astype(jnp.bfloat16)


def late_kernel(
    sizes, orders, raw_ref, taps_ref, dead_ref, sources_ref, table_ref,
    out_ref, fir_ref, alive_ref, band_ref, select_ref,
):
    windows, rows, _ = out_ref.shape
    fill_fir(taps_ref, fir_ref)
    fill_alive(dead_ref, alive_ref)
    fill_band(band_ref)
    fill_selector(sizes, orders, sources_ref, select_ref)
    samples = jnp.concatenate(
        [raw_ref[:, w * SPAN - TAPS : (w + 1) * SPAN] for w in range(1, windows + 1)], axis=0
    )
    dec = nt_dot(samples, fir_ref[...]).astype(jnp.bfloat16)
    alive = jnp.concatenate([alive_ref[...]] * windows, axis=0)
    out_ref[...] = whiten(dec, table_ref, band_ref, alive).reshape(out_ref.shape)


def pick(select, white):
    return jnp.dot(select, white, preferred_element_type=jnp.float32).astype(jnp.bfloat16)


def first_kernel(
    raw_ref, hist_ref, fir_ref, table_ref, band_ref, alive_ref, late_ref, select_ref,
    panel_ref, white_ref,
):
    white_ref[1:] = late_ref[...]
    samples = jnp.concatenate([hist_ref[...], raw_ref[:, :SPAN]], axis=1)
    dec = nt_dot(samples, fir_ref[...]).astype(jnp.bfloat16)
    white_ref[0] = whiten(dec, table_ref, band_ref, alive_ref[...])
    select = select_ref[: panel_ref.shape[1]]
    for w in range(white_ref.shape[0]):
        panel_ref[w] = pick(select, white_ref[w])


def panels_kernel(skip, groups, select_ref, white_ref, *refs):
    own_refs, other_refs = refs[: len(groups)], refs[len(groups) :]
    for w in range(white_ref.shape[0]):
        chosen = pick(select_ref[skip:], white_ref[w])
        row = 0
        for group, own_ref, other_ref in zip(groups, own_refs, other_refs):
            place = 0
            for count in group:
                own_ref[w, place : place + count] = chosen[row : row + count]
                other_ref[w, place : place + count] = chosen[row + count : row + 2 * count]
                row += 2 * count
                place += count


def merge_kernel(*refs):
    groups = len(refs) // 3
    for own_ref, sib_ref, panel_ref in zip(refs[:groups], refs[groups : 2 * groups], refs[2 * groups :]):
        panel_ref[0] = own_ref[...]
        panel_ref[1] = sib_ref[...]


def gate_kernel(table_ref, out_ref):
    out_ref[...] = jnp.zeros_like(out_ref)


def split_kernel(panel_ref, recv_ref, keep_ref, send_ref):
    count = keep_ref.shape[1]
    keep_ref[...] = panel_ref[:, :count] + recv_ref[:, :count]
    send_ref[...] = panel_ref[:, count:] + recv_ref[:, count:]


def product_kernel(sources, begin, white_ref, white_sib_ref, cos_ref, sin_ref, out_ref):
    windows = white_ref.shape[0]
    count = out_ref.shape[0]
    cos_lag = cos_ref[...][None]
    sin_lag = sin_ref[...][None]
    white = jnp.concatenate(
        [ref[w] for ref in (white_ref, white_sib_ref) for w in range(windows)], axis=1
    )
    parts = []
    for side in range(2):
        for w in range(windows):
            source = sources(side, w, begin // NLAG, count // NLAG)
            real_src = source[:, None, :HALF]
            imag_src = source[:, None, HALF:]
            for part in (
                real_src * cos_lag + imag_src * sin_lag,
                imag_src * cos_lag - real_src * sin_lag,
            ):
                parts.append(part.reshape(count, HALF).astype(jnp.bfloat16))
    out_ref[...] = nt_dot(jnp.concatenate(parts, axis=1), white).astype(out_ref.dtype)


def taken_kernel(first, own_ref, sib_ref, *refs):
    def sources(side, w, begin, count):
        return (own_ref, sib_ref)[side][w, begin : begin + count].astype(jnp.float32)

    product_kernel(sources, first, *refs)


def summed_kernel(place, first, panel_ref, recv_ref, *refs):
    def sources(side, w, begin, count):
        rows = slice(place + begin, place + begin + count)
        return panel_ref[side, w, rows].astype(jnp.float32) + recv_ref[side, w, rows].astype(jnp.float32)

    product_kernel(sources, first, *refs)


def halves_kernel(pieces, *refs):
    *parts, kept_ref, send_ref = refs
    place = 0
    for keep_ref, recv_ref, counts in zip(parts[::2], parts[1::2], pieces):
        row = 0
        for count in counts:
            half = count // 2
            for out_ref, begin in ((kept_ref, row), (send_ref, row + half)):
                rows = slice(begin, begin + half)
                value = keep_ref[rows, :] + recv_ref[rows, :].astype(jnp.float32)
                out_ref[place : place + half, :] = value.astype(out_ref.dtype)
            row += count
            place += half


def total_kernel(keep_ref, recv_ref, out_ref):
    out_ref[...] = keep_ref[...] + recv_ref[...].astype(jnp.float32)


def last_kernel(pieces, *refs):
    *parts, out_ref, late_ref, sems = refs
    parts = iter(parts)
    copies, place = [], 0
    for summed, places in sorted(pieces, key=lambda piece: not piece[0]):
        keep_ref = next(parts)
        recv_ref = None if summed else next(parts)
        row = 0
        for begin, count in places:
            source = keep_ref.at[row : row + count]
            if not summed:
                rows = slice(row, row + count)
                late_ref[place : place + count] = keep_ref[rows, :] + recv_ref[rows, :].astype(jnp.float32)
                source = late_ref.at[place : place + count]
                place += count
            copy = pltpu.make_async_copy(source, out_ref.at[begin : begin + count], sems.at[len(copies)])
            copy.start()
            copies.append(copy)
            row += count
    for copy in copies:
        copy.wait()


class Chain:
    def __init__(self):
        self.last = None

    def __call__(self, name, kernel, args, outs, scratch=(), gates=(), waits=(), limit=VMEM_LIMIT, first=VMEM, result=VMEM):
        args, gates = list(args), list(gates)
        order = [*waits] if self.last is None else [*waits, self.last]
        taken, passed = len(args), len(args) + len(gates) + len(order)

        def body(*refs):
            written = refs[passed : passed + len(outs)]
            kernel(*refs[:taken], *written, *refs[passed + len(outs) + len(gates) :])

        results = pl.pallas_call(
            body,
            out_shape=[*outs, *(jax.ShapeDtypeStruct(g.shape, g.dtype) for g in gates)],
            in_specs=[first] + [VMEM] * (taken - 1) + [ANY] * (len(gates) + len(order)),
            out_specs=[result] * len(outs) + [ANY] * len(gates),
            input_output_aliases={taken + i: len(outs) + i for i in range(len(gates))},
            scratch_shapes=list(scratch),
            compiler_params=params(limit),
            cost_estimate=cost(1e9 * COSTS.get(name, BASE_COST), 1e4),
            name=name,
        )(*args, *gates, *order)
        self.last = results[0]
        return results


def local(raw_traces, fir_taps, sources, dead_flags):
    rows, samples = raw_traces.shape
    windows = samples // SPAN
    late = windows - 1
    time_parts = lax.axis_size("tm")
    chan_parts = lax.axis_size("chan")
    per_dest = VS // time_parts
    codes = time_parts // 2
    bits = [1 << i for i in range(1, time_parts.bit_length() - 1)]
    sizes, firsts, seconds, thirds, plan = CHUNKS, FIRST, SECOND, THIRD, PLAN
    across_groups = ACROSS
    if per_dest != sum(CHUNKS) or len(bits) != 3:
        sizes, firsts = (per_dest // 2,) * 2, (0, 0)
        seconds = thirds = ((0,), (1,))
        across_groups = ((1,),)
        plan = [("split", 0, (), ()), ("merge", 0, (1,), ())]
        plan += [(kind, q, (), ()) for q in (0, 1) for kind in ("send", "keep")]
        final = "third" + "+" * (len(bits) - 3)
        plan += [(name, q, (), ()) for name in ("second", *(final[:5 + i] for i in range(len(final) - 4))) for q in (0, 1)]
    final = "third" + "+" * (len(bits) - 3)
    orders = [[bits[first], *bits[:first], *bits[first + 1 :]] for first in firsts]
    counts = [size * codes for size in sizes]
    bf16, f32 = jnp.bfloat16, jnp.float32
    shape = jax.ShapeDtypeStruct
    chain = Chain()

    (tail,) = chain(
        "history", history_kernel, [pltpu.with_memory_space_constraint(raw_traces, pltpu.HBM)], [shape((rows, TAPS), bf16)], [pltpu.SemaphoreType.DMA],
        first=ANY,
    )
    history = lax.ppermute(tail, "tm", [(i, i + 1) for i in range(time_parts - 1)])

    table = jnp.asarray(dft_table())
    late_white, fir, alive, band, select = chain(
        "late",
        functools.partial(late_kernel, sizes, orders),
        [raw_traces, fir_taps.reshape(1, -1), dead_flags.reshape(1, -1), sources.reshape(1, -1), table],
        [
            shape((late, rows, TD), bf16),
            shape((TD, SPAN + TAPS), bf16),
            shape((rows, HALF), f32),
            shape((TD, HALF), bf16),
            shape((VS, rows), bf16),
        ],
    )
    panel, white = chain(
        "first",
        first_kernel,
        [raw_traces, history, fir, table, band, alive, late_white, select],
        [shape((windows, 2 * counts[0], TD), bf16), shape((windows, rows, TD), bf16)],
    )
    _, white = chain("gate", gate_kernel, [table], [shape((8, HALF), f32)], gates=[white])
    white_sib = swap(white, "tm", 1)
    members = [[counts[chunk] for chunk in group] for group in across_groups]
    rest = [shape((windows, sum(group), TD), bf16) for group in members]
    parts = chain("panels", functools.partial(panels_kernel, 2 * counts[0], members), [select, white], rest + rest)
    own, sib = parts[: len(rest)], [swap(other, "tm", 1) for other in parts[len(rest) :]]
    tables = [jnp.asarray(t) for t in lag_tables(1.0 / math.sqrt(time_parts * windows * TD))]
    spectra = [white, white_sib, *tables]

    def across(panel):
        if chan_parts == 2:
            return swap(panel, "chan", 1)
        return lax.psum(panel, "chan") - panel

    panels = {0: panel}
    arrived = {}
    state, pieces, moved = {}, {}, {}
    for kind, q, leaving, waits in plan:
        name = f"{kind}_{q}"
        gates = [panels[g] for g in leaving if g in panels]
        held = [moved[key] for key in waits if key in moved]
        call = functools.partial(chain, name, gates=gates, waits=held)
        if kind == "split":
            half = shape((windows, counts[0], TD), bf16)
            keep, send, *let = call(split_kernel, [panel, across(panel)], [half, half])
            taken = [keep, swap(send, "tm", 1)]
        elif kind == "merge":
            totals = [sum(counts[chunk] for chunk in group) for group in across_groups]
            made = call(merge_kernel, [*own, *sib], [shape((2, windows, total, TD), bf16) for total in totals])
            panels.update(enumerate(made, 1))
            let = []
        elif kind in ("send", "keep"):
            half = counts[q] * NLAG // 2
            args, kernel = taken, taken_kernel
            for g, group in enumerate(across_groups, 1):
                if q in group:
                    place = sum(counts[chunk] for chunk in group if chunk < q)
                    args, kernel = [panels[g], arrived[g]], functools.partial(summed_kernel, place)
            made, *let = call(
                functools.partial(kernel, half if kind == "send" else 0), [*args, *spectra],
                [shape((half, rows), bf16 if kind == "send" else f32)],
            )
            if kind == "send":
                moved["first", q] = swap(made, "tm", orders[q][0])
                pieces["first", q] = [half]
            else:
                state["first", q] = made, moved["first", q]
        elif kind == "sum":
            keep, recv = state["third", q]
            total, *let = call(total_kernel, [keep, recv], [shape(keep.shape, f32)])
            state["third", q] = total, None
        else:
            before, groups = {"second": ("first", seconds), "third": ("second", thirds)}.get(kind, (kind[:-1], thirds))
            members = [(before, member) for member in groups[q]]
            if before.startswith("third"):
                members = [(before, q)]
            split = [pieces[m] for m in members]
            half = sum(map(sum, split)) // 2
            keep, send, *let = call(
                functools.partial(halves_kernel, split), [x for m in members for x in state[m]],
                [shape((half, rows), f32), shape((half, rows), bf16)],
            )
            pieces[kind, q] = [count // 2 for part in split for count in part]
            chunk = groups[q][0] if kind == "second" else seconds[groups[q][0]][0]
            stage = 1 if kind == "second" else 2 + kind.count("+")
            moved[kind, q] = swap(send, "tm", orders[chunk][stage])
            state[kind, q] = keep, moved[kind, q]
        panels.update(zip(leaving, let))
        for g in leaving:
            moved["y", g] = arrived[g] = across(panels[g])

    starts = [sum(sizes[:q]) * NLAG for q in range(len(sizes))]
    args, places = [], []
    for q, group in sorted(enumerate(thirds), key=lambda item: state[final, item[0]][1] is not None):
        args += [x for x in state[final, q] if x is not None]
        chunks = [chunk for member in group for chunk in seconds[member]]
        places.append((state[final, q][1] is None, [(starts[chunk], sizes[chunk] * NLAG) for chunk in chunks]))
    (stacked,) = chain(
        "last",
        functools.partial(last_kernel, places),
        args,
        [shape((per_dest * NLAG, rows), f32)],
        [pltpu.VMEM((per_dest * NLAG, rows), f32), pltpu.SemaphoreType.DMA((len(sizes),))],
        result=ANY,
    )
    return stacked.reshape(per_dest, NLAG, rows)


def solution(mesh):
    return jax.shard_map(
        local,
        mesh=mesh,
        in_specs=(P("chan", "tm"), P(), P(), P("chan")),
        out_specs=P("tm", None, "chan"),
        check_vma=False,
    )
```
